512 devices in a mesh: seq: 256 (over z, x, y_hi, core), head: 2 (over y_lo).
Axes of the slice: x: 4, y: 8 (y_hi: 4, y_lo: 2; y = y_hi * 2 + y_lo), z: 8, core: 2. Of those that a mesh axis runs over, the one named last changes fastest.
Arguments:
- queries: bfloat16 [65536, 2048], P('seq', 'head'), may hold values from -5 to 5
- key_rows: bfloat16 [65536, 2048], P('seq', 'head'), may hold values from -5 to 5
- value_rows: bfloat16 [65536, 2048], P('seq', 'head'), may hold values from -6 to 6
- out_grad: bfloat16 [65536, 2048], P('seq', 'head'), may hold values from -6 to 6
- padding: int32 [65536], P('seq'), may hold values 0 or 1
- header_keys: bfloat16 [256, 2048], P('seq', 'head'), may hold values from -6 to 6
- header_values: bfloat16 [256, 2048], P('seq', 'head'), may hold values from -6 to 6
- neighbours: int32 [512, 5], P('seq'), may hold values from 0 to 511, as said below
- slot_valid: int32 [512, 5], P('seq'), may hold values from 0 to 1, as said below
- crystal_ids: int32 [512], P('seq'), may hold values from 0 to 127, as said below
- header_index: int32 [128, 2], replicated, may hold values from 0 to 255, as said below
Outputs:
- query_grad: bfloat16 [65536, 2048], P(('seq', 'head'))
- key_grad: bfloat16 [65536, 2048], P(('seq', 'head'))
- value_grad: bfloat16 [65536, 2048], P(('seq', 'head'))
- header_key_grad: bfloat16 [256, 2048], P('seq', 'head')
- header_value_grad: bfloat16 [256, 2048], P('seq', 'head')
The draws below stay inside these ranges and needn't reach their ends.
Inputs may be any that keep to these rules, and one draw needn't show every extreme that they name: `crystal_ids`: crystals are runs of 3 to 5 consecutive token blocks, numbered in order from 0 at block 0; some crystal holds 5 blocks. `neighbours`: slot s of block b names the block of b's crystal at periodic offset 0, +1, -1, +2, -2 (s = 0 to 4) from b, counted modulo the crystal's number of blocks. `slot_valid`: 1 exactly on the first m slots of a block whose crystal holds m blocks. `header_index`: every header row is named by exactly one crystal.
All inputs are finite; a program needn't handle non-finite values. No bound on the sum of `padding` on one device may be relied on, other than what follows from the above.
Results may differ from the reference program's by a relative error of at most 0.0098.
Values may be sent and summed in bfloat16 or wider, within the bound.
A program may use at most 64 MiB of HBM per device.

```python
import math
import jax
import jax.numpy as jnp
import numpy as np
from jax import lax

HEADS = 16
DH = 128
BLK = 128
MOST = 5
BLK_DEV = 2
REACH = 2
TOK_DEV = 256
TOKENS = 65536
BLOCKS = 512
CRYST = 128
HDR = 256
N_SEQ = 256


def quad_table():
    combos = []
    for first_extra in range(3):
        for second_extra in range(3):
            for third_extra in range(3):
                fourth_extra = 4 - first_extra - second_extra - third_extra
                if 0 <= fourth_extra <= 2 and max(first_extra, second_extra, third_extra, fourth_extra) == 2:
                    combos.append([first_extra, second_extra, third_extra, fourth_extra])
    combos.append([1, 1, 1, 1])
    return jnp.array(np.array(combos, dtype=np.int32))


def crystal_layout(key):
    combos = quad_table()
    with_most = combos.shape[0] - 1
    chosen = jax.random.randint(jax.random.fold_in(key, 101), (CRYST // 4,), 0, with_most + 1)
    leading = jax.random.randint(jax.random.fold_in(key, 102), (), 0, with_most)
    chosen = chosen.at[0].set(leading).astype(jnp.int32)
    counts = (3 + jnp.take(combos, chosen, axis=0).reshape(CRYST)).astype(jnp.int32)
    ends = jnp.cumsum(counts).astype(jnp.int32)
    starts = ends - counts
    blocks = jnp.arange(BLOCKS, dtype=jnp.int32)
    ident = jnp.sum((blocks[:, None] >= ends[None, :]).astype(jnp.int32), axis=1).astype(jnp.int32)
    start_b = jnp.take(starts, ident)
    size_b = jnp.take(counts, ident)
    slots = jnp.arange(MOST, dtype=jnp.int32)
    offsets = (slots + 1) // 2 * jnp.where(slots % 2 == 1, 1, -1).astype(jnp.int32)
    local = blocks - start_b
    lists = start_b[:, None] + (local[:, None] + offsets[None, :]) % size_b[:, None]
    valid = (slots[None, :] < size_b[:, None]).astype(jnp.int32)
    return (ident, lists.astype(jnp.int32), valid)


def draw_queries(key, part):
    key = jax.random.fold_in(key, 1)
    values = jnp.clip(jax.random.normal(key, (TOKENS, HEADS * DH), jnp.float32), -4.0, 4.0)
    return values.astype(jnp.bfloat16)


def draw_key_rows(key, part):
    key = jax.random.fold_in(key, 2)
    values = jnp.clip(jax.random.normal(key, (TOKENS, HEADS * DH), jnp.float32), -4.0, 4.0)
    return values.astype(jnp.bfloat16)


def draw_crystal_ids(key, part):
    ident, lists, valid = crystal_layout(key)
    return ident


def draw_neighbours(key, part):
    ident, lists, valid = crystal_layout(key)
    return lists


def draw_slot_valid(key, part):
    ident, lists, valid = crystal_layout(key)
    return valid


def draw_header_index(key, part):
    key = jax.random.fold_in(key, 7)
    order = jax.random.permutation(key, jnp.arange(HDR, dtype=jnp.int32))
    return order.reshape(CRYST, 2).astype(jnp.int32)


def touch_ends(values, key, low, largest):
    longest = values.shape.index(max(values.shape))
    spots = []
    for shift in (0, 1):
        where = [jax.random.randint(jax.random.fold_in(key, axis), (), 0, length) for axis, length in enumerate(values.shape)]
        where[longest] = (where[longest] + shift) % values.shape[longest]
        spots.append(tuple(where))
    return values.at[spots[0]].set(low).at[spots[1]].set(largest)


def steps_of(key, shape, split, least, top_value):
    loudness = 1.0
    for dim, shards_of in split:
        heights = jax.random.uniform(jax.random.fold_in(jax.random.fold_in(key, 6), dim), (shards_of,), jnp.float32, least / len(split), top_value / len(split))
        loudness = loudness * jnp.repeat(jnp.exp(heights), shape[dim] // shards_of).reshape((-1,) + (1,) * (len(shape) - 1 - dim))
    return loudness


def scatter_about(own_key, dims, deviation, most, shards=(), kind=jnp.bfloat16):
    factor_of = steps_of(own_key, dims, shards, -0.22, 0.18) if shards else 1.0
    result = jax.random.normal(own_key, dims, jnp.float32) * deviation * factor_of
    return jnp.minimum(jnp.maximum(result, -most), most).astype(kind)


def setup_inputs(seed: int = 0) -> dict:
    seeds = jax.random.split(jax.random.key(seed), 12)
    return {
        "queries": draw_queries(jax.random.fold_in(seeds[11], 71), 0),
        "key_rows": draw_key_rows(jax.random.fold_in(seeds[11], 71), 0),
        "value_rows": scatter_about(seeds[2], (TOKENS, HEADS * DH), 1.0, 6.0, ((0, 256), (1, 2))),
        "out_grad": scatter_about(seeds[3], (TOKENS, HEADS * DH), 1.0, 6.0, ((0, 256), (1, 2))),
        "padding": touch_ends((jax.random.randint(seeds[4], (TOKENS,), 0, 8) < 7).astype(jnp.int32), jax.random.fold_in(seeds[4], 1), 0, 1),
        "header_keys": scatter_about(seeds[5], (HDR, HEADS * DH), 1.0, 6.0, ((0, 256), (1, 2))),
        "header_values": scatter_about(seeds[6], (HDR, HEADS * DH), 1.0, 6.0, ((0, 256), (1, 2))),
        "neighbours": draw_neighbours(jax.random.fold_in(seeds[11], 71), 0),
        "slot_valid": draw_slot_valid(jax.random.fold_in(seeds[11], 71), 0),
        "crystal_ids": draw_crystal_ids(jax.random.fold_in(seeds[11], 71), 0),
        "header_index": draw_header_index(jax.random.fold_in(seeds[11], 71), 0),
    }


NEG_SCORE = -1e+30
HIGH = lax.Precision.HIGHEST

def block_terms(query_dev, grad_dev, key_all, value_all, allowed, factor):
    qf = query_dev.astype(jnp.float32)
    gf = grad_dev.astype(jnp.float32)
    kf = key_all.astype(jnp.float32)
    vf = value_all.astype(jnp.float32)
    score = jnp.einsum('bqhe,bkhe->bhqk', qf, kf, precision=HIGH) * factor
    score = jnp.where(allowed[:, None, None, :], score, NEG_SCORE)
    top = lax.optimization_barrier(jnp.max(score, axis=-1, keepdims=True))
    total = lax.optimization_barrier(jnp.sum(jnp.exp(score - top), axis=-1, keepdims=True))
    prob = jnp.exp(score - (top + jnp.log(total)))
    prob_low = prob.astype(jnp.bfloat16).astype(jnp.float32)
    attended = jnp.einsum('bhqk,bkhe->bqhe', prob_low, vf, precision=HIGH)
    delta = lax.optimization_barrier(jnp.sum(gf * attended, axis=-1))
    delta = jnp.transpose(delta, (0, 2, 1))[..., None]
    dprob = jnp.einsum('bqhe,bkhe->bhqk', gf, vf, precision=HIGH)
    mixing = (factor * prob * (dprob - delta)).astype(jnp.bfloat16).astype(jnp.float32)
    q_grad = jnp.einsum('bhqk,bkhe->bqhe', mixing, kf, precision=HIGH)
    k_grad = jnp.einsum('bhqk,bqhe->bkhe', mixing, qf, precision=HIGH)
    v_grad = jnp.einsum('bhqk,bqhe->bkhe', prob_low, gf, precision=HIGH)
    return (q_grad, k_grad, v_grad)

def reference(queries, key_rows, value_rows, out_grad, padding, header_keys, header_values, neighbours, slot_valid, crystal_ids, header_index):
    width = HEADS * DH
    span = (2 * REACH + 1) * BLK_DEV
    factor = 1.0 / math.sqrt(DH)

    def one_device(carry, place):
        key_acc, value_acc, head_key_acc, head_value_acc = carry
        first = (place - REACH) * BLK_DEV % BLOCKS
        win_rows = ((first * BLK + jnp.arange(span * BLK, dtype=jnp.int32)) % TOKENS).astype(jnp.int32)
        win_key = jnp.take(key_rows, win_rows, axis=0).reshape(span, BLK, width)
        win_value = jnp.take(value_rows, win_rows, axis=0).reshape(span, BLK, width)
        win_pad = jnp.take(padding, win_rows, axis=0).reshape(span, BLK)
        block_start = (place * BLK_DEV).astype(jnp.int32)
        lists = lax.dynamic_slice_in_dim(neighbours, block_start, BLK_DEV, 0)
        valid = lax.dynamic_slice_in_dim(slot_valid, block_start, BLK_DEV, 0)
        ids = lax.dynamic_slice_in_dim(crystal_ids, block_start, BLK_DEV, 0)
        local = ((lists - first) % BLOCKS).astype(jnp.int32)
        rows = jnp.take(header_index, ids, axis=0).reshape(-1).astype(jnp.int32)
        head_key = jnp.take(header_keys, rows, axis=0).reshape(BLK_DEV, 2, HEADS, DH)
        head_value = jnp.take(header_values, rows, axis=0).reshape(BLK_DEV, 2, HEADS, DH)
        slot_keys = jnp.take(win_key, local, axis=0).reshape(BLK_DEV, MOST * BLK, HEADS, DH)
        slot_values = jnp.take(win_value, local, axis=0).reshape(BLK_DEV, MOST * BLK, HEADS, DH)
        key_all = jnp.concatenate([slot_keys, head_key], axis=1)
        value_all = jnp.concatenate([slot_values, head_value], axis=1)
        slot_ok = (jnp.take(win_pad, local, axis=0) > 0) & (valid[:, :, None] > 0)
        allowed = jnp.concatenate([slot_ok.reshape(BLK_DEV, MOST * BLK), jnp.ones((BLK_DEV, 2), dtype=bool)], axis=1)
        tok_start = (place * TOK_DEV).astype(jnp.int32)
        query_dev = lax.dynamic_slice_in_dim(queries, tok_start, TOK_DEV, 0).reshape(BLK_DEV, BLK, HEADS, DH)
        grad_dev = lax.dynamic_slice_in_dim(out_grad, tok_start, TOK_DEV, 0).reshape(BLK_DEV, BLK, HEADS, DH)
        q_grad, k_grad, v_grad = block_terms(query_dev, grad_dev, key_all, value_all, allowed, factor)
        onehot = (local[:, :, None] == jnp.arange(span, dtype=jnp.int32)[None, None, :]).astype(jnp.float32)

        def to_window(grad):
            slots = grad[:, :MOST * BLK].reshape(BLK_DEV, MOST, BLK, width)
            return jnp.einsum('bsw,bskf->wkf', onehot, slots, precision=HIGH).reshape(span * BLK, width)
        low_key, low_value = lax.optimization_barrier((to_window(k_grad).astype(jnp.bfloat16), to_window(v_grad).astype(jnp.bfloat16)))
        key_acc = key_acc.at[win_rows].add(low_key.astype(jnp.float32))
        value_acc = value_acc.at[win_rows].add(low_value.astype(jnp.float32))
        head_key_acc = head_key_acc.at[rows].add(k_grad[:, MOST * BLK:].reshape(BLK_DEV * 2, width))
        head_value_acc = head_value_acc.at[rows].add(v_grad[:, MOST * BLK:].reshape(BLK_DEV * 2, width))
        return ((key_acc, value_acc, head_key_acc, head_value_acc), q_grad.reshape(TOK_DEV, width).astype(jnp.bfloat16))
    init = (jnp.zeros((TOKENS, width), jnp.float32), jnp.zeros((TOKENS, width), jnp.float32), jnp.zeros((HDR, width), jnp.float32), jnp.zeros((HDR, width), jnp.float32))
    carry, q_parts = lax.scan(one_device, init, jnp.arange(N_SEQ, dtype=jnp.int32))
    key_acc, value_acc, head_key_acc, head_value_acc = carry
    return (q_parts.reshape(TOKENS, width), key_acc.astype(jnp.bfloat16), value_acc.astype(jnp.bfloat16), head_key_acc.astype(jnp.bfloat16), head_value_acc.astype(jnp.bfloat16))
```

```python
import math

import jax
import jax.numpy as jnp
from jax import lax
from jax.experimental import pallas as pl
from jax.experimental.pallas import tpu as pltpu
from jax.sharding import PartitionSpec as P

DH = 128
BLK = 128
NEG = -1e30
FACTOR = 1.0 / math.sqrt(DH)
F32 = jnp.float32
BF16 = jnp.bfloat16
HD = 4
WIN = 1024
KEYS = WIN + 16
HROW = 512
SEQ = 256


def kernel(
    q_in, g_in, k_in, v_in, meta_in, hdr_in, hidx,
    q_out, k_out, v_out, h_out,
    qg, kv, bias, probs, mixes, grads, back, meta, meta_s, table, hb, hd, htab, rz, sz, rx, sx, ry,
    f_send, f_recv, own_sem, b_send, b_recv, bown_sem, m_send, m_recv, ms_sem,
    hs_send, hs_recv, ht_send, ht_recv,
):
    e = lax.axis_index("seq")
    h = lax.axis_index("head")
    core = lax.rem(e, 2)
    chip = e // 2
    j8 = lax.rem(e, 8)
    x4 = lax.rem(e // 8, 4)
    z8 = e // 32

    def wrap(index):
        return lax.rem(index + SEQ, SEQ)

    step = 2 * core - 1
    peer = e + 1 - 2 * core
    near = wrap(e + step)
    far = wrap(e + 2 * step)
    far_from = wrap(e - 2 * step)
    after = wrap(2 * chip + 2)
    before = wrap(2 * chip - 1)

    def y_peer(d):
        return e - j8 + lax.rem(j8 + d, 8)

    def x_peer(d):
        return e - 8 * x4 + 8 * lax.rem(x4 + d, 4)

    def z_peer(d):
        return e - 32 * z8 + 32 * lax.rem(z8 + d, 8)

    barrier = pltpu.get_barrier_semaphore()

    def greet(device, other):
        pl.semaphore_signal(barrier, inc=1, device_id=(device, other), device_id_type=pl.DeviceIdType.MESH)

    for d in range(1, 8):
        greet(y_peer(d), h)
        greet(z_peer(d), h)
    for d in range(1, 4):
        greet(x_peer(d), h)
    greet(near, h)
    greet(far_from, h)
    greet(e, 1 - h)
    greet(peer, 1 - h)
    next_chip = wrap(2 * (chip + step))
    for other in range(2):
        greet(next_chip, other)
        greet(next_chip + 1, other)

    def remote(src, dst, send, recv, device, other):
        return pltpu.make_async_remote_copy(
            src_ref=src, dst_ref=dst, send_sem=send, recv_sem=recv,
            device_id=(device, other), device_id_type=pl.DeviceIdType.MESH,
        )

    table[pl.ds(e, 1)] = hdr_in[...][None]
    meta[pl.ds(1 + core, 1)] = meta_in[...][None]

    pl.semaphore_wait(barrier, 25)

    def row_y(d):
        return remote(table.at[e], table.at[e], hs_send.at[d - 1], hs_recv.at[d - 1], y_peer(d), h)

    def row_x(d):
        part = table.at[pl.ds(e - j8, 8)]
        return remote(part, part, hs_send.at[6 + d], hs_recv.at[6 + d], x_peer(d), h)

    def row_z(d):
        part = table.at[pl.ds(32 * z8, 32)]
        return remote(part, part, hs_send.at[9 + d], hs_recv.at[9 + d], z_peer(d), h)

    for d in range(1, 8):
        row_y(d).start()

    ext_slot = 3 - 3 * core
    targets = ((peer, 1 - core, 1 + core), (near, 1 - core, ext_slot), (far, core, ext_slot))

    def meta_copy(kind):
        device, _, slot = targets[kind]
        return remote(meta.at[1 + core], meta.at[slot], m_send.at[kind], m_recv.at[kind], device, h)

    for kind in range(3):
        meta_copy(kind).start()

    def key_row(slot):
        return pl.multiple_of(slot * 256 + 16 * (slot // 2), 16)

    def place(array, head, slot):
        if array < 2:
            return qg.at[head, array, pl.ds(pl.multiple_of(slot * 256, 256), 256)]
        return kv.at[head, array - 2, pl.ds(key_row(slot), 256)]

    ins = (q_in, g_in, k_in, v_in)

    def forward(kind, array, head):
        device, group, slot = targets[kind]
        cols = pl.ds(pl.multiple_of((group * HD + head) * DH, DH), DH)
        return remote(
            ins[array].at[:, cols], place(array, head, slot),
            f_send.at[head, kind, array], f_recv.at[head, kind, array], device, h,
        )

    def own_copy(array, head):
        cols = pl.ds(pl.multiple_of((core * HD + head) * DH, DH), DH)
        return pltpu.make_async_copy(ins[array].at[:, cols], place(array, head, 1 + core), own_sem.at[head, array])

    def send_head(head, carry):
        for array in range(4):
            for kind in range(3):
                forward(kind, array, head).start()
            own_copy(array, head).start()
        return carry

    send_head(0, 0)
    for d in range(1, 8):
        row_y(d).wait_recv()
    for d in range(1, 4):
        row_x(d).start()
    for d in range(1, 4):
        row_x(d).wait_recv()
    for d in range(1, 8):
        row_z(d).start()
    lax.fori_loop(1, HD, send_head, 0)

    for kind in range(3):
        meta_copy(kind).wait_recv()
    to_scalar = pltpu.make_async_copy(meta, meta_s, ms_sem)
    to_scalar.start()
    to_scalar.wait()
    id_x = meta_s[1, 2, 0]
    id_y = meta_s[2, 3, 0]
    for pair in range(4):
        ids = jnp.concatenate([meta[pair, 2:3, :], meta[pair, 3:4, :]], axis=1).astype(F32)
        for block in range(8):
            codes = meta[block // 2, block % 2 : block % 2 + 1, :].astype(F32)
            codes = jnp.broadcast_to(codes, (BLK, BLK)).T
            codes = jnp.concatenate([codes, codes], axis=1)
            row = block * BLK + 16 * (block // 4)
            bias[pair, row : row + BLK, :] = jnp.where(codes == ids, 0.0, NEG)
        rows = lax.broadcasted_iota(jnp.int32, (16, 256), 0)
        both = jnp.where(rows < 2, id_x, jnp.where((rows < 4) & (id_x != id_y), id_y, -2))
        bias[pair, HROW : HROW + 16, :] = jnp.where(both.astype(F32) == ids, 0.0, NEG)
    probs[784:1040, 0:256] = jnp.zeros((256, 256), BF16)
    mixes[784:1040, 0:256] = jnp.zeros((256, 256), BF16)
    probs[0:256, 768:1024] = jnp.zeros((256, 256), BF16)
    mixes[0:256, 768:1024] = jnp.zeros((256, 256), BF16)

    for d in range(1, 8):
        row_z(d).wait_recv()
    rows_x = (hidx[2 * id_x], hidx[2 * id_x + 1])
    rows_y = (hidx[2 * id_y], hidx[2 * id_y + 1])
    for slot, row in enumerate(rows_x + rows_y):
        hb[slot] = table[row].astype(F32)
    for head in range(HD):
        for array in range(2):
            at = pl.ds(array * 8 + core * HD + head, 1)
            lines = [hb[slot, at, :] for slot in range(4)] + [jnp.zeros((12, DH), F32)]
            kv[head, array, HROW : HROW + 16, :] = jnp.concatenate(lines, axis=0).astype(BF16)

    mine = 2 * core + h

    def ret(which, head):
        col = pl.ds(pl.multiple_of(h * 1024 + (core * HD + head) * DH, DH), DH)
        if which < 3:
            there = lax.rem(mine + which + 1, 4)
            device, other, block, sem = 2 * chip + there // 2, lax.rem(there, 2), 2 + there, which
            side = 0
        else:
            other = (which - 3) % 2
            block = (6, 7, 0, 1)[which - 3]
            device = after if which < 5 else before
            side = 1
            sem = 3 + mine
        src = grads.at[head, :, pl.ds(block * BLK, BLK), :]
        return remote(src, back.at[side, :, :, col], b_send.at[head, which], b_recv.at[head, sem], device, other)

    def ret_wait(which, head):
        col = pl.ds(pl.multiple_of(h * 1024 + (core * HD + head) * DH, DH), DH)
        src = grads.at[head, :, pl.ds(0, BLK), :]
        dst = back.at[0 if which < 3 else 1, :, :, col]
        remote(src, dst, b_send.at[head, which], b_recv.at[head, which], peer, h).wait_recv()

    def ret_own(head):
        col = pl.ds(pl.multiple_of(h * 1024 + (core * HD + head) * DH, DH), DH)
        src = grads.at[head, :, pl.ds(pl.multiple_of((2 + mine) * BLK, BLK), BLK), :]
        return pltpu.make_async_copy(src, back.at[0, :, :, col], bown_sem.at[head])

    def nt(a, b):
        return lax.dot_general(a, b, (((1,), (1,)), ((), ())), preferred_element_type=F32)

    def work(head, carry):
        for array in range(4):
            for kind in range(3):
                forward(kind, array, head).wait_recv()
            own_copy(array, head).wait()
        for pair in range(4):
            lo, hi = (0, 784) if pair == 0 else (256, KEYS) if pair == 3 else (0, KEYS)
            cols = slice(pair * 256, pair * 256 + 256)
            q = qg[head, 0, cols, :]
            g = qg[head, 1, cols, :]
            keys = kv[head, 0, lo:hi, :]
            values = kv[head, 1, lo:hi, :]
            score = nt(keys, q) * FACTOR + bias[pair, lo:hi, :]
            top = jnp.max(score, axis=0, keepdims=True)
            grown = jnp.exp(score - top)
            prob = grown * (1.0 / jnp.sum(grown, axis=0, keepdims=True))
            low = prob.astype(BF16)
            dprob = nt(values, g)
            delta = jnp.sum(low.astype(F32) * dprob, axis=0, keepdims=True)
            mixing = (FACTOR * prob * (dprob - delta)).astype(BF16)
            probs[lo:hi, cols] = low
            mixes[lo:hi, cols] = mixing
            q_grad = lax.dot_general(mixing, keys, (((0,), (0,)), ((), ())), preferred_element_type=F32)
            grads[head, 0, cols, :] = q_grad.astype(BF16)
        for array, weights in ((1, mixes), (2, probs)):
            total = jnp.dot(weights[...], qg[head, array - 1], preferred_element_type=F32)
            grads[head, array, 0:512, :] = total[0:512].astype(BF16)
            grads[head, array, 512:1024, :] = total[528:1040].astype(BF16)
            for slot in range(4):
                hd[slot, pl.ds((array - 1) * HD + head, 1), :] = total[HROW + slot : HROW + slot + 1]
        for which in range(7):
            ret(which, head).start()
        ret_own(head).start()
        return carry

    lax.fori_loop(0, HD, work, 0)

    home_x = meta_s[1, 4, 0] == chip
    home_y = (meta_s[2, 5, 0] == chip) & (id_x != id_y)
    names = [jnp.where(home_x, row, -1) for row in rows_x] + [jnp.where(home_y, row, -1) for row in rows_y]

    def fill(row, carry):
        total = jnp.zeros((8, DH), F32)
        for slot in range(4):
            total = total + jnp.where(names[slot] == row, hd[slot], 0.0)
        htab[pl.ds(row, 1)] = total[None]
        return carry

    lax.fori_loop(0, SEQ, fill, 0)

    def out_z(d):
        src = htab.at[pl.ds(32 * lax.rem(z8 + d, 8), 32)]
        return remote(src, rz.at[d - 1], ht_send.at[d - 1], ht_recv.at[d - 1], z_peer(d), h)

    def out_x(d):
        src = sz.at[pl.ds(8 * lax.rem(x4 + d, 4), 8)]
        return remote(src, rx.at[d - 1], ht_send.at[6 + d], ht_recv.at[6 + d], x_peer(d), h)

    def out_y(d):
        src = sx.at[lax.rem(j8 + d, 8)]
        return remote(src, ry.at[j8], ht_send.at[9 + d], ht_recv.at[9 + d], y_peer(d), h)

    for d in range(1, 8):
        out_z(d).start()
    for d in range(1, 8):
        out_z(d).wait_recv()
    total = htab[pl.ds(32 * z8, 32)]
    for d in range(7):
        total = total + rz[d]
    sz[...] = total
    for d in range(1, 4):
        out_x(d).start()
    for d in range(1, 4):
        out_x(d).wait_recv()
    total = sz[pl.ds(8 * x4, 8)]
    for d in range(3):
        total = total + rx[d]
    sx[...] = total
    for d in range(1, 8):
        out_y(d).start()
    ry[pl.ds(j8, 1)] = sx[pl.ds(j8, 1)]
    for d in range(1, 8):
        out_y(d).wait_recv()
    halves = [ry[c] + ry[c + 2] + ry[c + 4] + ry[c + 6] for c in range(2)]
    lines = [halves[0][0:4], halves[1][0:4], halves[0][4:8], halves[1][4:8]]
    h_out[...] = jnp.concatenate(lines, axis=0).astype(BF16)

    def settle(head, carry):
        for which in range(7):
            ret_wait(which, head)
        ret_own(head).wait()
        return carry

    lax.fori_loop(0, HD, settle, 0)
    here = meta_s[1 + core, 4 + h, 0] == chip
    for array, out in ((0, q_out), (1, k_out), (2, v_out)):
        out[...] = jnp.where(here, back[0, array], back[1, array])

    def drain(head, carry):
        for array in range(4):
            for kind in range(3):
                forward(kind, array, head).wait_send()
        for which in range(7):
            ret(which, head).wait_send()
        return carry

    lax.fori_loop(0, HD, drain, 0)
    for kind in range(3):
        meta_copy(kind).wait_send()
    for d in range(1, 8):
        row_y(d).wait_send()
        row_z(d).wait_send()
        out_y(d).wait_send()
        out_z(d).wait_send()
    for d in range(1, 4):
        row_x(d).wait_send()
        out_x(d).wait_send()


def body(
    queries, key_rows, value_rows, out_grad, padding, header_keys, header_values,
    neighbours, slot_valid, crystal_ids, header_index,
):
    used = slot_valid > 0
    size = jnp.sum(used.astype(jnp.int32), axis=1)
    start = jnp.min(jnp.where(used, neighbours, 1 << 20), axis=1)
    first = start // 4
    left = jnp.minimum(4 * first + 4 - start, size)
    home = first + ((left < size) & (left <= 2)).astype(jnp.int32)
    ids = crystal_ids[:, None]
    codes = jnp.where(padding.reshape(2, BLK) > 0, ids, -1)
    wide = (2, BLK)
    meta = jnp.concatenate(
        [codes, jnp.broadcast_to(ids, wide), jnp.broadcast_to(home[:, None], wide), jnp.zeros(wide, jnp.int32)]
    )
    hdr = jnp.concatenate([header_keys.reshape(8, DH), header_values.reshape(8, DH)])
    grad = jax.ShapeDtypeStruct((BLK, 2048), BF16)
    vmem = pl.BlockSpec(memory_space=pltpu.VMEM)
    hbm = pl.BlockSpec(memory_space=pl.ANY)
    dma = pltpu.SemaphoreType.DMA
    q_grad, k_grad, v_grad, h_grad = pl.pallas_call(
        kernel,
        out_shape=(grad, grad, grad, jax.ShapeDtypeStruct((16, DH), BF16)),
        in_specs=[hbm] * 4 + [vmem] * 2 + [pl.BlockSpec(memory_space=pltpu.SMEM)],
        out_specs=[vmem] * 4,
        scratch_shapes=[
            pltpu.VMEM((HD, 2, WIN, DH), BF16),
            pltpu.VMEM((HD, 2, KEYS, DH), BF16),
            pltpu.VMEM((4, KEYS, 256), F32),
            pltpu.VMEM((KEYS, WIN), BF16),
            pltpu.VMEM((KEYS, WIN), BF16),
            pltpu.VMEM((HD, 3, WIN, DH), BF16),
            pltpu.VMEM((2, 3, BLK, 2048), BF16),
            pltpu.VMEM((4, 8, BLK), jnp.int32),
            pltpu.SMEM((4, 8, BLK), jnp.int32),
            pltpu.VMEM((SEQ, 16, DH), BF16),
            pltpu.VMEM((4, 16, DH), F32),
            pltpu.VMEM((4, 8, DH), F32),
            pltpu.VMEM((SEQ, 8, DH), F32),
            pltpu.VMEM((7, 32, 8, DH), F32),
            pltpu.VMEM((32, 8, DH), F32),
            pltpu.VMEM((3, 8, 8, DH), F32),
            pltpu.VMEM((8, 8, DH), F32),
            pltpu.VMEM((8, 8, DH), F32),
            dma((HD, 3, 4)),
            dma((HD, 3, 4)),
            dma((HD, 4)),
            dma((HD, 7)),
            dma((HD, 7)),
            dma((HD,)),
            dma((3,)),
            dma((3,)),
            dma,
            dma((17,)),
            dma((17,)),
            dma((17,)),
            dma((17,)),
        ],
        compiler_params=pltpu.CompilerParams(
            collective_id=0, has_side_effects=True, vmem_limit_bytes=56 * 1024 * 1024
        ),
    )(queries, out_grad, key_rows, value_rows, meta, hdr, header_index.reshape(-1))
    return (q_grad, k_grad, v_grad, h_grad[:8].reshape(1, 1024), h_grad[8:].reshape(1, 1024))


def solution(mesh):
    in_specs = (
        P("seq", "head"),
        P("seq", "head"),
        P("seq", "head"),
        P("seq", "head"),
        P("seq"),
        P("seq", "head"),
        P("seq", "head"),
        P("seq", None),
        P("seq", None),
        P("seq"),
        P(),
    )
    out_specs = (
        P(("seq", "head"), None),
        P(("seq", "head"), None),
        P(("seq", "head"), None),
        P("seq", "head"),
        P("seq", "head"),
    )
    return jax.shard_map(body, mesh=mesh, in_specs=in_specs, out_specs=out_specs, check_vma=False)
```

```python
import math

import jax
import jax.numpy as jnp
from jax import lax
from jax.experimental import pallas as pl
from jax.experimental.pallas import tpu as pltpu
from jax.sharding import PartitionSpec as P

DH = 128
BLK = 128
NEG = -1e30
FACTOR = 1.0 / math.sqrt(DH)
F32 = jnp.float32
BF16 = jnp.bfloat16
HD = 4
MOST = 5
ROWS = MOST * BLK
KEYS = ROWS + 16
SEQ = 256
CAP = (6, 4)
CHUNKS = ((0, 256), (256, 512), (512, 640))


def kernel(
    q_in, g_in, k_in, v_in, meta_in, hdr_in, hidx,
    q_out, k_out, v_out, h_out,
    wk, sbuf, land, imp, cqg, ckv, probs, mixes, bias, gr, rsend, rland, rw, ost, back,
    meta, meta_s, padw, tabf, table, hb, hd, hz, hx, hs, ry,
    e_send, e_recv, own_sem, f_send, f_recv, r_send, r_recv, x_send, x_recv, xown_sem,
    m_send, m_recv, ms_sem, hs_send, hs_recv, ht_send, ht_recv,
):
    e = lax.axis_index("seq")
    h = lax.axis_index("head")
    core = lax.rem(e, 2)
    chip = e // 2
    j8 = lax.rem(e, 8)
    x4 = lax.rem(e // 8, 4)
    z8 = e // 32

    def wrap(index):
        return lax.rem(index + SEQ, SEQ)

    step = 2 * core - 1
    peer = e + 1 - 2 * core
    sends_to = (wrap(e + 2 * step), wrap(e - 2 * step))
    comes_from = (sends_to[1], sends_to[0])
    left, right = wrap(2 * chip - 2), wrap(2 * chip + 2)

    def y_peer(d):
        return e - j8 + lax.rem(j8 + d, 8)

    def x_peer(d):
        return e - 8 * x4 + 8 * lax.rem(x4 + d, 4)

    def z_peer(d):
        return e - 32 * z8 + 32 * lax.rem(z8 + d, 8)

    barrier = pltpu.get_barrier_semaphore()

    def greet(device, other):
        pl.semaphore_signal(barrier, inc=1, device_id=(device, other), device_id_type=pl.DeviceIdType.MESH)

    for d in range(1, 8):
        greet(y_peer(d), h)
        greet(z_peer(d), h)
    for d in range(1, 4):
        greet(x_peer(d), h)
    for c in range(2):
        greet(left + c, h)
        greet(right + c, h)
    greet(e, 1 - h)
    greet(peer, 1 - h)

    def remote(src, dst, send, recv, device, other):
        return pltpu.make_async_remote_copy(
            src_ref=src, dst_ref=dst, send_sem=send, recv_sem=recv,
            device_id=(device, other), device_id_type=pl.DeviceIdType.MESH,
        )

    ins = (q_in, g_in, k_in, v_in)

    def own_copy(array, head):
        cols = pl.ds(pl.multiple_of((core * HD + head) * DH, DH), DH)
        there = wk.at[head, array, pl.ds(2 * core, 2)]
        return pltpu.make_async_copy(ins[array].at[:, :, cols], there, own_sem.at[head, array])

    def peer_copy(array, head):
        cols = pl.ds(pl.multiple_of(((1 - core) * HD + head) * DH, DH), DH)
        there = wk.at[head, array, pl.ds(2 * core, 2)]
        return remote(ins[array].at[:, :, cols], there, e_send.at[head, array], e_recv.at[head, array], peer, h)

    tabf[pl.ds(j8, 1)] = hdr_in[...][None]
    meta[pl.ds(2 + core, 1)] = meta_in[...][None]
    for array in range(4):
        for head in range(HD):
            own_copy(array, head).start()

    pl.semaphore_wait(barrier, 23)

    meta_to = ((peer, 2 + core), (left, 4 + core), (left + 1, 4 + core), (right, core), (right + 1, core))

    def meta_copy(kind):
        device, slot = meta_to[kind]
        return remote(meta.at[2 + core], meta.at[slot], m_send.at[kind], m_recv.at[slot], device, h)

    def meta_arrival(slot):
        return remote(meta.at[2 + core], meta.at[slot], m_send.at[0], m_recv.at[slot], peer, h)

    for kind in range(5):
        meta_copy(kind).start()

    def row_y(d):
        return remote(tabf.at[j8], tabf.at[j8], hs_send.at[d - 1], hs_recv.at[d - 1], y_peer(d), h)

    def row_x(d):
        part = table.at[pl.ds(4 * (4 * z8 + x4), 4)]
        return remote(part, part, hs_send.at[6 + d], hs_recv.at[6 + d], x_peer(d), h)

    def row_z(d):
        part = table.at[pl.ds(16 * z8, 16)]
        return remote(part, part, hs_send.at[9 + d], hs_recv.at[9 + d], z_peer(d), h)

    for d in range(1, 8):
        row_y(d).start()
    for array in range(4):
        for head in range(HD):
            peer_copy(array, head).start()

    for slot in (0, 1, 4, 5):
        meta_arrival(slot).wait_recv()
    meta_arrival(3 - core).wait_recv()
    to_scalar = pltpu.make_async_copy(meta, meta_s, ms_sem)
    to_scalar.start()
    to_scalar.wait()
    start_x, size_x, id_x = meta_s[2, 2, 0] - 4 * chip, meta_s[2, 4, 0], meta_s[2, 6, 0]
    start_y, size_y, id_y = meta_s[3, 3, 0] - 4 * chip, meta_s[3, 5, 0], meta_s[3, 7, 0]
    a_x = jnp.maximum(-start_x, 0)
    b_x = size_x - a_x
    b_y = jnp.maximum(start_y + size_y - 4, 0)
    a_y = size_y - b_y
    cross_x, cross_y = a_x > 0, b_y > 0
    same = id_x == id_y
    on_x = jnp.logical_not(same & cross_y)
    on_y = jnp.logical_not(same) | cross_y

    def left_heads(a, b):
        return jnp.where(b == 1, 3, jnp.where(a == 1, 1, jnp.where(b == 2, 3 - core, 2 - core)))

    split_x, split_y = left_heads(a_x, b_x), left_heads(a_y, b_y)

    def home_x(head):
        return jnp.logical_not(cross_x) | (head >= split_x)

    def home_y(head):
        return jnp.logical_not(cross_y) | (head < split_y)

    is_x = (core == 1, core == 0)

    def pick(unit, of_x, of_y):
        return jnp.where(is_x[unit], of_x, of_y)

    start_u = [pick(u, start_x, start_y) for u in range(2)]
    size_u = [pick(u, size_x, size_y) for u in range(2)]
    width_u = [pick(u, a_x, b_y) for u in range(2)]
    given_u = [pick(u, b_x, a_y) for u in range(2)]
    id_u = [pick(u, id_x, id_y) for u in range(2)]
    on_u = [pick(u, on_x, on_y) for u in range(2)]

    def over(slot, width):
        by = [slot // n for n in range(1, 5)]
        return jnp.where(width == 2, by[1], jnp.where(width == 3, by[2], jnp.where(width == 4, by[3], by[0])))

    def rest(slot, width):
        return slot - over(slot, width) * jnp.clip(width, 1, 4)

    for d in range(1, 8):
        row_y(d).wait_recv()
    rows = tabf[...].astype(F32)
    halves = [
        jnp.concatenate([rows[:, HD * c : HD * c + HD], rows[:, 8 + HD * c : 8 + HD * c + HD]], axis=1)
        for c in range(2)
    ]
    rows = jnp.where(core == 0, halves[0], halves[1])
    table[pl.ds(4 * (4 * z8 + x4), 4)] = rows.reshape(4, 16, DH).astype(BF16)
    for d in range(1, 4):
        row_x(d).start()

    for array in range(4):
        for head in range(HD):
            own_copy(array, head).wait()
            peer_copy(array, head).wait_recv()

    def forward(d, slot):
        at = 6 * d + slot
        return remote(sbuf.at[at], land.at[at], f_send.at[at], f_recv.at[at], sends_to[d], h)

    def send(d, slot):
        unit = 1 - d
        width = given_u[unit]
        order = jnp.clip(over(slot, width), 0, HD - 1)
        part = rest(slot, width)
        head = pick(unit, order, HD - 1 - order)
        block = jnp.clip(pick(unit, part, 4 - a_y + part), 0, 3)
        sbuf[6 * d + slot] = wk[head, :, block]
        forward(d, slot).start()

    for slot in range(4):
        for d in range(2):
            send(d, slot)
    for d in range(1, 4):
        row_x(d).wait_recv()
    for d in range(1, 8):
        row_z(d).start()
    for slot in range(4, 6):
        send(0, slot)

    for slot in range(6):
        for block in range(2):
            padw[2 * slot + block] = jnp.broadcast_to(meta[slot, block : block + 1, :].astype(F32), (8, BLK))
    for u in range(2):
        for p in range(MOST):
            line = padw[jnp.clip(start_u[u] + p + 4, 0, 11)][0:1]
            full = jnp.broadcast_to(line, (BLK, BLK)).T
            full = jnp.where(p < size_u[u], full, 0.0)
            bias[u, p * BLK : p * BLK + BLK, :] = jnp.where(full > 0.0, 0.0, NEG)
        at = lax.broadcasted_iota(jnp.int32, (16, BLK), 0)
        bias[u, ROWS:KEYS, :] = jnp.where(at < 2, 0.0, NEG)

    for d in range(1, 8):
        row_z(d).wait_recv()
    names = []
    for u in range(2):
        for slot in range(2):
            row = hidx[2 * id_u[u] + slot]
            pair = table[lax.div(row, 2)].astype(F32)
            hb[2 * u + slot] = jnp.where(lax.rem(row, 2) == 0, pair[0:8], pair[8:16])
            names.append(jnp.where(on_u[u], row, -1))

    def nt(a, b):
        return lax.dot_general(a, b, (((1,), (1,)), ((), ())), preferred_element_type=F32)

    def give_back(d, slot):
        at = 6 * d + slot
        return remote(rsend.at[at], rland.at[at], r_send.at[at], r_recv.at[at], comes_from[d], h)

    def send_back(d, slot):
        part = rest(slot, width_u[d])
        turn = jnp.clip(over(slot, width_u[d]), 0, HD - 1)
        p = jnp.clip(pick(d, part, part + 4 - start_u[d]), 0, MOST - 1)
        rsend[6 * d + slot] = gr[d, turn, :, p]
        give_back(d, slot).start()

    def work(turn, carry):
        @pl.when(turn == 0)
        def _():
            for slot in range(4):
                for d in range(2):
                    forward(d, slot).wait_recv()
                    imp[6 * d + slot] = land[6 * d + slot]

        @pl.when(turn == 1)
        def _():
            for slot in range(4, 6):
                forward(0, slot).wait_recv()
                imp[slot] = land[slot]

        for u in range(2):
            head = turn + (core if u == 0 else 1 - core) * (HD - 1 - 2 * turn)
            last = jnp.where(turn == 0, 3, CAP[u] - 1)
            for p in range(MOST):
                there = start_u[u] + p
                slot = turn * width_u[u] + pick(u, p, there - 4)
                outside = (there < 0) | (there > 3)
                far = imp[6 * u + jnp.clip(slot, 0, last)]
                near = wk[head, :, jnp.clip(there, 0, 3)]
                rows = jnp.where(outside, far, near)
                span = slice(p * BLK, p * BLK + BLK)
                cqg[u, :, span, :] = jnp.where(p < size_u[u], rows[0:2], jnp.zeros_like(rows[0:2]))
                ckv[u, :, span, :] = rows[2:4]
            for array in range(2):
                at = pl.ds(array * HD + head, 1)
                lines = [hb[2 * u + slot, at, :] for slot in range(2)] + [jnp.zeros((14, DH), F32)]
                ckv[u, array, ROWS:KEYS, :] = jnp.concatenate(lines, axis=0).astype(BF16)
            for lo, hi in CHUNKS:
                q = cqg[u, 0, lo:hi, :]
                g = cqg[u, 1, lo:hi, :]
                keys = ckv[u, 0]
                values = ckv[u, 1]
                mask = bias[u]
                if hi - lo == 256:
                    mask = jnp.concatenate([mask, mask], axis=1)
                score = nt(keys, q) * FACTOR + mask
                top = jnp.max(score, axis=0, keepdims=True)
                grown = jnp.exp(score - top)
                prob = grown * (1.0 / jnp.sum(grown, axis=0, keepdims=True))
                low = prob.astype(BF16)
                dprob = nt(values, g)
                delta = jnp.sum(low.astype(F32) * dprob, axis=0, keepdims=True)
                mixing = (FACTOR * prob * (dprob - delta)).astype(BF16)
                probs[u, :, lo:hi] = low
                mixes[u, :, lo:hi] = mixing
                q_grad = lax.dot_general(mixing, keys, (((0,), (0,)), ((), ())), preferred_element_type=F32)
                gr[u, turn, 0, lo // BLK : hi // BLK] = q_grad.astype(BF16).reshape(-1, BLK, DH)
            here = pick(u, home_x(head), home_y(head))
            for array, weights in ((0, mixes), (1, probs)):
                total = jnp.dot(weights[u], cqg[u, array], preferred_element_type=F32)
                gr[u, turn, 1 + array] = total[0:ROWS].astype(BF16).reshape(MOST, BLK, DH)
                for slot in range(2):
                    line = total[ROWS + slot : ROWS + slot + 1]
                    hd[2 * u + slot, pl.ds(array * HD + head, 1), :] = jnp.where(here, line, 0.0)

        for ready, slots in ((0, (0,)), (1, (1, 3)), (2, (2, 4, 5))):

            @pl.when(turn == ready)
            def _(slots=slots):
                for slot in slots:
                    for d in range(2):
                        if slot < CAP[d]:
                            send_back(d, slot)

        return carry

    lax.fori_loop(0, HD, work, 0)

    tags = [jnp.full((1, DH), name).astype(F32) for name in names] + [jnp.full((12, DH), -1.0, F32)]
    block = jnp.concatenate([hd[slot] for slot in range(4)] + tags, axis=0)
    hz[pl.ds(z8, 1)] = block.astype(BF16)[None]

    def out_z(d):
        return remote(hz.at[z8], hz.at[z8], ht_send.at[d - 1], ht_recv.at[d - 1], z_peer(d), h)

    def out_x(d):
        return remote(hx.at[x4], hx.at[x4], ht_send.at[6 + d], ht_recv.at[6 + d], x_peer(d), h)

    def out_y(d):
        src = hs.at[lax.rem(j8 + d, 8)]
        return remote(src, ry.at[j8], ht_send.at[9 + d], ht_recv.at[9 + d], y_peer(d), h)

    for d in range(1, 8):
        out_z(d).start()

    mine = 2 * core + h

    def column(head):
        return pl.ds(pl.multiple_of(h * 1024 + (core * HD + head) * DH, DH), DH)

    def deliver(d, head):
        there = lax.rem(mine + d, 4)
        return remote(
            ost.at[head, there], back.at[:, :, column(head)], x_send.at[head, d - 1], x_recv.at[head, d - 1],
            2 * chip + there // 2, lax.rem(there, 2),
        )

    def keep(head):
        return pltpu.make_async_copy(ost.at[head, mine], back.at[:, :, column(head)], xown_sem.at[head])

    for d in range(2):
        for slot in range(CAP[d]):
            give_back(d, slot).wait_recv()
            rw[6 * d + slot] = rland[6 * d + slot]
    unit_x = jnp.where(core == 1, 0, 1)

    def assemble(head, carry):
        for j in range(4):
            in_x = on_x & (j < start_x + size_x)
            unit = jnp.where(in_x, unit_x, 1 - unit_x)
            turn = jnp.where(in_x, HD - 1 - head, head)
            p = jnp.clip(jnp.where(in_x, j - start_x, j - start_y), 0, MOST - 1)
            slot = jnp.where(in_x, head * b_x + j, (HD - 1 - head) * a_y + j - start_y)
            here = jnp.where(in_x, home_x(head).astype(jnp.int32), home_y(head).astype(jnp.int32)) > 0
            most = jnp.where(unit == 1, CAP[0] - 1, CAP[1] - 1)
            at = 6 * (1 - unit) + jnp.clip(slot, 0, most)
            worked = gr[unit, turn, :, p]
            ost[head, j] = jnp.where(here, worked, rw[at])
        for d in range(1, 4):
            deliver(d, head).start()
        keep(head).start()
        return carry

    lax.fori_loop(0, HD, assemble, 0)

    for d in range(1, 8):
        out_z(d).wait_recv()
    hx[pl.ds(x4, 1)] = hz[...].reshape(1, 8 * 48, DH)
    for d in range(1, 4):
        out_x(d).start()
    for d in range(1, 4):
        out_x(d).wait_recv()
    first = 32 * z8 + 8 * x4

    def gather(at, totals):
        block = hx[at // 8, pl.ds(pl.multiple_of(lax.rem(at, 8) * 48, 16), 48), :].astype(F32)
        totals = list(totals)
        for slot in range(4):
            tag = jnp.broadcast_to(block[32 + slot : 33 + slot], (8, DH)) - first.astype(F32)
            for j in range(8):
                totals[j] = totals[j] + jnp.where(tag == float(j), block[8 * slot : 8 * slot + 8], 0.0)
        return tuple(totals)

    totals = lax.fori_loop(0, 32, gather, tuple(jnp.zeros((8, DH), F32) for _ in range(8)))
    for j in range(8):
        hs[j] = totals[j]
    for d in range(1, 8):
        out_y(d).start()
    ry[pl.ds(j8, 1)] = hs[pl.ds(j8, 1)]
    for d in range(1, 8):
        out_y(d).wait_recv()
    halves = [ry[c] + ry[c + 2] + ry[c + 4] + ry[c + 6] for c in range(2)]
    lines = [halves[0][0:4], halves[1][0:4], halves[0][4:8], halves[1][4:8]]
    h_out[...] = jnp.concatenate(lines, axis=0).astype(BF16)

    def settle(head, carry):
        for d in range(1, 4):
            deliver(d, head).wait_recv()
        keep(head).wait()
        return carry

    lax.fori_loop(0, HD, settle, 0)
    for array, out in ((0, q_out), (1, k_out), (2, v_out)):
        out[...] = back[array]

    for array in range(4):
        for head in range(HD):
            peer_copy(array, head).wait_send()
    for d in range(2):
        for slot in range(CAP[d]):
            forward(d, slot).wait_send()
            give_back(d, slot).wait_send()
    for head in range(HD):
        for d in range(1, 4):
            deliver(d, head).wait_send()
    for kind in range(5):
        meta_copy(kind).wait_send()
    for d in range(1, 8):
        row_y(d).wait_send()
        row_z(d).wait_send()
        out_y(d).wait_send()
        out_z(d).wait_send()
    for d in range(1, 4):
        row_x(d).wait_send()
        out_x(d).wait_send()


def body(
    queries, key_rows, value_rows, out_grad, padding, header_keys, header_values,
    neighbours, slot_valid, crystal_ids, header_index,
):
    used = slot_valid > 0
    size = jnp.sum(used.astype(jnp.int32), axis=1)
    start = jnp.min(jnp.where(used, neighbours, 1 << 20), axis=1)
    wide = [jnp.broadcast_to(each[:, None], (2, BLK)) for each in (start, size, crystal_ids)]
    meta = jnp.concatenate([padding.reshape(2, BLK)] + wide)
    hdr = jnp.concatenate([header_keys.reshape(8, DH), header_values.reshape(8, DH)])
    grad = jax.ShapeDtypeStruct((BLK, 2048), BF16)
    vmem = pl.BlockSpec(memory_space=pltpu.VMEM)
    hbm = pl.BlockSpec(memory_space=pl.ANY)
    dma = pltpu.SemaphoreType.DMA
    q_grad, k_grad, v_grad, h_grad = pl.pallas_call(
        kernel,
        out_shape=(grad, grad, grad, jax.ShapeDtypeStruct((16, DH), BF16)),
        in_specs=[hbm] * 4 + [vmem] * 2 + [pl.BlockSpec(memory_space=pltpu.SMEM)],
        out_specs=[vmem] * 4,
        scratch_shapes=[
            pltpu.VMEM((HD, 4, 4, BLK, DH), BF16),
            pltpu.VMEM((10, 4, BLK, DH), BF16),
            pltpu.VMEM((10, 4, BLK, DH), BF16),
            pltpu.VMEM((10, 4, BLK, DH), BF16),
            pltpu.VMEM((2, 2, ROWS, DH), BF16),
            pltpu.VMEM((2, 2, KEYS, DH), BF16),
            pltpu.VMEM((2, KEYS, ROWS), BF16),
            pltpu.VMEM((2, KEYS, ROWS), BF16),
            pltpu.VMEM((2, KEYS, BLK), F32),
            pltpu.VMEM((2, HD, 3, MOST, BLK, DH), BF16),
            pltpu.VMEM((10, 3, BLK, DH), BF16),
            pltpu.VMEM((10, 3, BLK, DH), BF16),
            pltpu.VMEM((10, 3, BLK, DH), BF16),
            pltpu.VMEM((HD, 4, 3, BLK, DH), BF16),
            pltpu.VMEM((3, BLK, 2048), BF16),
            pltpu.VMEM((6, 8, BLK), jnp.int32),
            pltpu.SMEM((6, 8, BLK), jnp.int32),
            pltpu.VMEM((12, 8, BLK), F32),
            pltpu.VMEM((8, 16, DH), BF16),
            pltpu.VMEM((SEQ // 2, 16, DH), BF16),
            pltpu.VMEM((4, 8, DH), F32),
            pltpu.VMEM((4, 8, DH), F32),
            pltpu.VMEM((8, 48, DH), BF16),
            pltpu.VMEM((4, 8 * 48, DH), BF16),
            pltpu.VMEM((8, 8, DH), F32),
            pltpu.VMEM((8, 8, DH), F32),
            dma((HD, 4)),
            dma((HD, 4)),
            dma((HD, 4)),
            dma((10,)),
            dma((10,)),
            dma((10,)),
            dma((10,)),
            dma((HD, 3)),
            dma((HD, 3)),
            dma((HD,)),
            dma((5,)),
            dma((6,)),
            dma,
            dma((17,)),
            dma((17,)),
            dma((17,)),
            dma((17,)),
        ],
        compiler_params=pltpu.CompilerParams(
            collective_id=0, has_side_effects=True, vmem_limit_bytes=56 * 1024 * 1024
        ),
    )(*[each.reshape(2, BLK, 1024) for each in (queries, out_grad, key_rows, value_rows)], meta, hdr, header_index.reshape(-1))
    return (q_grad, k_grad, v_grad, h_grad[:8].reshape(1, 1024), h_grad[8:].reshape(1, 1024))


def solution(mesh):
    in_specs = (
        P("seq", "head"),
        P("seq", "head"),
        P("seq", "head"),
        P("seq", "head"),
        P("seq"),
        P("seq", "head"),
        P("seq", "head"),
        P("seq", None),
        P("seq", None),
        P("seq"),
        P(),
    )
    out_specs = (
        P(("seq", "head"), None),
        P(("seq", "head"), None),
        P(("seq", "head"), None),
        P("seq", "head"),
        P("seq", "head"),
    )
    return jax.shard_map(body, mesh=mesh, in_specs=in_specs, out_specs=out_specs, check_vma=False)
```

```python
import math

import jax
import jax.numpy as jnp
from jax import lax
from jax.experimental import pallas as pl
from jax.experimental.pallas import tpu as pltpu
from jax.sharding import PartitionSpec as P

DH = 128
BLK = 128
NEG = -1e30
FACTOR = 1.0 / math.sqrt(DH)
F32 = jnp.float32
BF16 = jnp.bfloat16
HD = 4
MOST = 5
ROWS = MOST * BLK
KEYS = ROWS + 16
SEQ = 256
CAP = (6, 4)
CHUNKS = ((0, 256), (256, 512), (512, 640))


def kernel(
    q_in, g_in, k_in, v_in, pad_in, hk_in, hv_in, lists, valid, ids, hidx,
    q_out, k_out, v_out, h_out,
    wk, sbuf, land, imp, cqg, ckv, probs, mixes, bias, gr, rsend, rland, rw, ost, back,
    meta, meta_s, padw, tabf, table, hb, hd, hz, hx, hs, ry,
    e_send, e_recv, own_sem, f_send, f_recv, r_send, r_recv, x_send, x_recv, xown_sem,
    m_send, m_recv, ms_sem, hs_send, hs_recv, ht_send, ht_recv,
):
    e = lax.axis_index("seq")
    h = lax.axis_index("head")
    core = lax.rem(e, 2)
    chip = e // 2
    j8 = lax.rem(e, 8)
    x4 = lax.rem(e // 8, 4)
    z8 = e // 32

    def wrap(index):
        return lax.rem(index + SEQ, SEQ)

    step = 2 * core - 1
    peer = e + 1 - 2 * core
    sends_to = (wrap(e + 2 * step), wrap(e - 2 * step))
    comes_from = (sends_to[1], sends_to[0])
    left, right = wrap(2 * chip - 2), wrap(2 * chip + 2)

    def y_peer(d):
        return e - j8 + lax.rem(j8 + d, 8)

    def x_peer(d):
        return e - 8 * x4 + 8 * lax.rem(x4 + d, 4)

    def z_peer(d):
        return e - 32 * z8 + 32 * lax.rem(z8 + d, 8)

    barrier = pltpu.get_barrier_semaphore()

    def greet(device, other):
        pl.semaphore_signal(barrier, inc=1, device_id=(device, other), device_id_type=pl.DeviceIdType.MESH)

    for d in range(1, 8):
        greet(y_peer(d), h)
        greet(z_peer(d), h)
    for d in range(1, 4):
        greet(x_peer(d), h)
    for c in range(2):
        greet(left + c, h)
        greet(right + c, h)
    greet(e, 1 - h)
    greet(peer, 1 - h)

    def remote(src, dst, send, recv, device, other):
        return pltpu.make_async_remote_copy(
            src_ref=src, dst_ref=dst, send_sem=send, recv_sem=recv,
            device_id=(device, other), device_id_type=pl.DeviceIdType.MESH,
        )

    ins = (q_in, g_in, k_in, v_in)

    def own_copy(array, head):
        cols = pl.ds(pl.multiple_of((core * HD + head) * DH, DH), DH)
        there = wk.at[head, array, pl.ds(2 * core, 2)]
        return pltpu.make_async_copy(ins[array].at[:, :, cols], there, own_sem.at[head, array])

    def peer_copy(array, head):
        cols = pl.ds(pl.multiple_of(((1 - core) * HD + head) * DH, DH), DH)
        there = wk.at[head, array, pl.ds(2 * core, 2)]
        return remote(ins[array].at[:, :, cols], there, e_send.at[head, array], e_recv.at[head, array], peer, h)

    for array in range(4):
        for head in range(HD):
            own_copy(array, head).start()
    lines = [each[:, DH * i : DH * i + DH] for each in (hk_in, hv_in) for i in range(8)]
    tabf[pl.ds(j8, 1)] = jnp.concatenate([line.astype(F32) for line in lines], axis=0).astype(BF16)[None]
    starts, sizes = [], []
    for block in range(2):
        first, size = jnp.int32(1 << 20), jnp.int32(0)
        for slot in range(MOST):
            used = valid[block, slot] > 0
            first = jnp.where(used, jnp.minimum(first, lists[block, slot]), first)
            size = size + jnp.where(used, 1, 0)
        starts.append(first)
        sizes.append(size)
    lines = [jnp.full((1, BLK), each, jnp.int32) for each in starts + sizes + [ids[0], ids[1]]]
    meta[pl.ds(2 + core, 1)] = jnp.concatenate([pad_in[...]] + lines, axis=0)[None]

    pl.semaphore_wait(barrier, 23)

    meta_to = ((peer, 2 + core), (left, 4 + core), (left + 1, 4 + core), (right, core), (right + 1, core))

    def meta_copy(kind):
        device, slot = meta_to[kind]
        return remote(meta.at[2 + core], meta.at[slot], m_send.at[kind], m_recv.at[slot], device, h)

    def meta_arrival(slot):
        return remote(meta.at[2 + core], meta.at[slot], m_send.at[0], m_recv.at[slot], peer, h)


    def row_y(d):
        return remote(tabf.at[j8], tabf.at[j8], hs_send.at[d - 1], hs_recv.at[d - 1], y_peer(d), h)

    def row_x(d):
        part = table.at[pl.ds(4 * (4 * z8 + x4), 4)]
        return remote(part, part, hs_send.at[6 + d], hs_recv.at[6 + d], x_peer(d), h)

    def row_z(d):
        part = table.at[pl.ds(16 * z8, 16)]
        return remote(part, part, hs_send.at[9 + d], hs_recv.at[9 + d], z_peer(d), h)

    for d in range(1, 8):
        row_y(d).start()
    for kind in range(5):
        meta_copy(kind).start()
    for array in range(4):
        for head in range(HD):
            peer_copy(array, head).start()

    for d in range(1, 8):
        row_y(d).wait_recv()
    rows = tabf[...].astype(F32)
    halves = [
        jnp.concatenate([rows[:, HD * c : HD * c + HD], rows[:, 8 + HD * c : 8 + HD * c + HD]], axis=1)
        for c in range(2)
    ]
    rows = jnp.where(core == 0, halves[0], halves[1])
    table[pl.ds(4 * (4 * z8 + x4), 4)] = rows.reshape(4, 16, DH).astype(BF16)
    for d in range(1, 4):
        row_x(d).start()

    for slot in (0, 1, 4, 5):
        meta_arrival(slot).wait_recv()
    meta_arrival(3 - core).wait_recv()
    to_scalar = pltpu.make_async_copy(meta, meta_s, ms_sem)
    to_scalar.start()
    for d in range(1, 4):
        row_x(d).wait_recv()
    for d in range(1, 8):
        row_z(d).start()
    to_scalar.wait()
    start_x, size_x, id_x = meta_s[2, 2, 0] - 4 * chip, meta_s[2, 4, 0], meta_s[2, 6, 0]
    start_y, size_y, id_y = meta_s[3, 3, 0] - 4 * chip, meta_s[3, 5, 0], meta_s[3, 7, 0]
    a_x = jnp.maximum(-start_x, 0)
    b_x = size_x - a_x
    b_y = jnp.maximum(start_y + size_y - 4, 0)
    a_y = size_y - b_y
    cross_x, cross_y = a_x > 0, b_y > 0
    same = id_x == id_y
    on_x = jnp.logical_not(same & cross_y)
    on_y = jnp.logical_not(same) | cross_y

    def left_heads(a, b):
        return jnp.where(b == 1, 3, jnp.where(a == 1, 1, jnp.where(b == 2, 3 - core, 2 - core)))

    split_x, split_y = left_heads(a_x, b_x), left_heads(a_y, b_y)

    def home_x(head):
        return jnp.logical_not(cross_x) | (head >= split_x)

    def home_y(head):
        return jnp.logical_not(cross_y) | (head < split_y)

    is_x = (core == 1, core == 0)

    def pick(unit, of_x, of_y):
        return jnp.where(is_x[unit], of_x, of_y)

    start_u = [pick(u, start_x, start_y) for u in range(2)]
    size_u = [pick(u, size_x, size_y) for u in range(2)]
    width_u = [pick(u, a_x, b_y) for u in range(2)]
    given_u = [pick(u, b_x, a_y) for u in range(2)]
    id_u = [pick(u, id_x, id_y) for u in range(2)]
    on_u = [pick(u, on_x, on_y) for u in range(2)]

    def over(slot, width):
        by = [slot // n for n in range(1, 5)]
        return jnp.where(width == 2, by[1], jnp.where(width == 3, by[2], jnp.where(width == 4, by[3], by[0])))

    def rest(slot, width):
        return slot - over(slot, width) * jnp.clip(width, 1, 4)

    for array in range(4):
        for head in range(HD):
            own_copy(array, head).wait()
            peer_copy(array, head).wait_recv()

    def forward(d, slot):
        at = 6 * d + slot
        return remote(sbuf.at[at], land.at[at], f_send.at[at], f_recv.at[at], sends_to[d], h)

    def send(d, slot):
        unit = 1 - d
        width = given_u[unit]
        order = jnp.clip(over(slot, width), 0, HD - 1)
        part = rest(slot, width)
        head = pick(unit, order, HD - 1 - order)
        block = jnp.clip(pick(unit, part, 4 - a_y + part), 0, 3)
        sbuf[6 * d + slot] = wk[head, :, block]
        forward(d, slot).start()

    for slot in range(4):
        for d in range(2):
            send(d, slot)
    for slot in range(4, 6):
        send(0, slot)

    for slot in range(6):
        for block in range(2):
            padw[2 * slot + block] = jnp.broadcast_to(meta[slot, block : block + 1, :].astype(F32), (8, BLK))
    for u in range(2):
        for p in range(MOST):
            line = padw[jnp.clip(start_u[u] + p + 4, 0, 11)][0:1]
            full = jnp.broadcast_to(line, (BLK, BLK)).T
            full = jnp.where(p < size_u[u], full, 0.0)
            bias[u, p * BLK : p * BLK + BLK, :] = jnp.where(full > 0.0, 0.0, NEG)
        at = lax.broadcasted_iota(jnp.int32, (16, BLK), 0)
        bias[u, ROWS:KEYS, :] = jnp.where(at < 2, 0.0, NEG)

    for d in range(1, 8):
        row_z(d).wait_recv()
    names = []
    for u in range(2):
        for slot in range(2):
            row = hidx[slot, id_u[u]]
            pair = table[lax.div(row, 2)].astype(F32)
            hb[2 * u + slot] = jnp.where(lax.rem(row, 2) == 0, pair[0:8], pair[8:16])
            names.append(jnp.where(on_u[u], row, -1))

    def nt(a, b):
        return lax.dot_general(a, b, (((1,), (1,)), ((), ())), preferred_element_type=F32)

    def give_back(d, slot):
        at = 6 * d + slot
        return remote(rsend.at[at], rland.at[at], r_send.at[at], r_recv.at[at], comes_from[d], h)

    def send_back(d, slot):
        part = rest(slot, width_u[d])
        turn = jnp.clip(over(slot, width_u[d]), 0, HD - 1)
        p = jnp.clip(pick(d, part, part + 4 - start_u[d]), 0, MOST - 1)
        rsend[6 * d + slot] = gr[d, turn, :, p]
        give_back(d, slot).start()

    def work(turn, carry):
        @pl.when(turn == 0)
        def _():
            for slot in range(4):
                for d in range(2):
                    forward(d, slot).wait_recv()
                    imp[6 * d + slot] = land[6 * d + slot]

        @pl.when(turn == 1)
        def _():
            for slot in range(4, 6):
                forward(0, slot).wait_recv()
                imp[slot] = land[slot]

        for u in range(2):
            head = turn + (core if u == 0 else 1 - core) * (HD - 1 - 2 * turn)
            last = jnp.where(turn == 0, 3, CAP[u] - 1)
            for p in range(MOST):
                there = start_u[u] + p
                slot = turn * width_u[u] + pick(u, p, there - 4)
                outside = (there < 0) | (there > 3)
                far = imp[6 * u + jnp.clip(slot, 0, last)]
                near = wk[head, :, jnp.clip(there, 0, 3)]
                rows = jnp.where(outside, far, near)
                span = slice(p * BLK, p * BLK + BLK)
                cqg[u, :, span, :] = jnp.where(p < size_u[u], rows[0:2], jnp.zeros_like(rows[0:2]))
                ckv[u, :, span, :] = rows[2:4]
            for array in range(2):
                at = pl.ds(array * HD + head, 1)
                lines = [hb[2 * u + slot, at, :] for slot in range(2)] + [jnp.zeros((14, DH), F32)]
                ckv[u, array, ROWS:KEYS, :] = jnp.concatenate(lines, axis=0).astype(BF16)
            for lo, hi in CHUNKS:
                q = cqg[u, 0, lo:hi, :]
                g = cqg[u, 1, lo:hi, :]
                keys = ckv[u, 0]
                values = ckv[u, 1]
                mask = bias[u]
                if hi - lo == 256:
                    mask = jnp.concatenate([mask, mask], axis=1)
                score = nt(keys, q) * FACTOR + mask
                top = jnp.max(score, axis=0, keepdims=True)
                grown = jnp.exp(score - top)
                prob = grown * (1.0 / jnp.sum(grown, axis=0, keepdims=True))
                low = prob.astype(BF16)
                dprob = nt(values, g)
                delta = jnp.sum(low.astype(F32) * dprob, axis=0, keepdims=True)
                mixing = (FACTOR * prob * (dprob - delta)).astype(BF16)
                probs[u, :, lo:hi] = low
                mixes[u, :, lo:hi] = mixing
                q_grad = lax.dot_general(mixing, keys, (((0,), (0,)), ((), ())), preferred_element_type=F32)
                gr[u, turn, 0, lo // BLK : hi // BLK] = q_grad.astype(BF16).reshape(-1, BLK, DH)
            here = pick(u, home_x(head), home_y(head))
            for array, weights in ((0, mixes), (1, probs)):
                total = jnp.dot(weights[u], cqg[u, array], preferred_element_type=F32)
                gr[u, turn, 1 + array] = total[0:ROWS].astype(BF16).reshape(MOST, BLK, DH)
                for slot in range(2):
                    line = total[ROWS + slot : ROWS + slot + 1]
                    hd[2 * u + slot, pl.ds(array * HD + head, 1), :] = jnp.where(here, line, 0.0)

        for ready, slots in ((0, (0,)), (1, (1, 3)), (2, (2, 4, 5))):

            @pl.when(turn == ready)
            def _(slots=slots):
                for slot in slots:
                    for d in range(2):
                        if slot < CAP[d]:
                            send_back(d, slot)

        return carry

    lax.fori_loop(0, HD, work, 0)

    tags = [jnp.full((1, DH), name).astype(F32) for name in names] + [jnp.full((12, DH), -1.0, F32)]
    block = jnp.concatenate([hd[slot] for slot in range(4)] + tags, axis=0)
    hz[pl.ds(z8, 1)] = block.astype(BF16)[None]

    def out_z(d):
        return remote(hz.at[z8], hz.at[z8], ht_send.at[d - 1], ht_recv.at[d - 1], z_peer(d), h)

    def out_x(d):
        return remote(hx.at[x4], hx.at[x4], ht_send.at[6 + d], ht_recv.at[6 + d], x_peer(d), h)

    def out_y(d):
        src = hs.at[lax.rem(j8 + d, 8)]
        return remote(src, ry.at[j8], ht_send.at[9 + d], ht_recv.at[9 + d], y_peer(d), h)

    for d in range(1, 8):
        out_z(d).start()

    mine = 2 * core + h

    def column(head):
        return pl.ds(pl.multiple_of(h * 1024 + (core * HD + head) * DH, DH), DH)

    def deliver(d, head):
        there = lax.rem(mine + d, 4)
        return remote(
            ost.at[head, there], back.at[:, :, column(head)], x_send.at[head, d - 1], x_recv.at[head, d - 1],
            2 * chip + there // 2, lax.rem(there, 2),
        )

    def keep(head):
        return pltpu.make_async_copy(ost.at[head, mine], back.at[:, :, column(head)], xown_sem.at[head])

    for slot in range(4):
        for d in range(2):
            give_back(d, slot).wait_recv()
            rw[6 * d + slot] = rland[6 * d + slot]
    unit_x = jnp.where(core == 1, 0, 1)

    def assemble(head, carry):
        for j in range(4):
            in_x = on_x & (j < start_x + size_x)
            unit = jnp.where(in_x, unit_x, 1 - unit_x)
            when = jnp.where(in_x, HD - 1 - head, head)
            p = jnp.clip(jnp.where(in_x, j - start_x, j - start_y), 0, MOST - 1)
            slot = jnp.where(in_x, head * b_x + j, (HD - 1 - head) * a_y + j - start_y)
            here = jnp.where(in_x, home_x(head).astype(jnp.int32), home_y(head).astype(jnp.int32)) > 0
            most = jnp.where(unit == 1, CAP[0] - 1, CAP[1] - 1)
            at = 6 * (1 - unit) + jnp.clip(slot, 0, most)
            worked = gr[unit, when, :, p]
            ost[head, j] = jnp.where(here, worked, rw[at])
        for d in range(1, 4):
            deliver(d, head).start()
        keep(head).start()
        return carry

    def assemble_pair(one, two):
        lax.fori_loop(0, 2, lambda i, carry: assemble(one + (two - one) * i, carry), 0)

    assemble_pair(0, 3)
    for slot in range(4, 6):
        give_back(0, slot).wait_recv()
        rw[slot] = rland[slot]
    assemble_pair(1, 2)

    for d in range(1, 8):
        out_z(d).wait_recv()
    hx[pl.ds(x4, 1)] = hz[...].reshape(1, 8 * 48, DH)
    for d in range(1, 4):
        out_x(d).start()
    for d in range(1, 4):
        out_x(d).wait_recv()
    first = 32 * z8 + 8 * x4

    def gather(at, totals):
        block = hx[at // 8, pl.ds(pl.multiple_of(lax.rem(at, 8) * 48, 16), 48), :].astype(F32)
        totals = list(totals)
        for slot in range(4):
            tag = jnp.broadcast_to(block[32 + slot : 33 + slot], (8, DH)) - first.astype(F32)
            for j in range(8):
                totals[j] = totals[j] + jnp.where(tag == float(j), block[8 * slot : 8 * slot + 8], 0.0)
        return tuple(totals)

    totals = lax.fori_loop(0, 32, gather, tuple(jnp.zeros((8, DH), F32) for _ in range(8)))
    for j in range(8):
        hs[j] = totals[j]
    for d in range(1, 8):
        out_y(d).start()
    ry[pl.ds(j8, 1)] = hs[pl.ds(j8, 1)]
    for d in range(1, 8):
        out_y(d).wait_recv()
    halves = [ry[c] + ry[c + 2] + ry[c + 4] + ry[c + 6] for c in range(2)]
    lines = [halves[0][0:4], halves[1][0:4], halves[0][4:8], halves[1][4:8]]
    h_out[...] = jnp.concatenate(lines, axis=0).astype(BF16)

    def settle(head, carry):
        for d in range(1, 4):
            deliver(d, head).wait_recv()
        keep(head).wait()
        return carry

    lax.fori_loop(0, HD, settle, 0)
    for array, out in ((0, q_out), (1, k_out), (2, v_out)):
        out[...] = back[array]

    for array in range(4):
        for head in range(HD):
            peer_copy(array, head).wait_send()
    for d in range(2):
        for slot in range(CAP[d]):
            forward(d, slot).wait_send()
            give_back(d, slot).wait_send()
    for head in range(HD):
        for d in range(1, 4):
            deliver(d, head).wait_send()
    for kind in range(5):
        meta_copy(kind).wait_send()
    for d in range(1, 8):
        row_y(d).wait_send()
        row_z(d).wait_send()
        out_y(d).wait_send()
        out_z(d).wait_send()
    for d in range(1, 4):
        row_x(d).wait_send()
        out_x(d).wait_send()


def finish(q_in, k_in, v_in, h_in, q_out, k_out, v_out, hk_out, hv_out):
    q_out[...] = q_in[...]
    k_out[...] = k_in[...]
    v_out[...] = v_in[...]
    rows = h_in[...].astype(F32)
    for i in range(8):
        hk_out[:, DH * i : DH * i + DH] = rows[i : i + 1].astype(BF16)
        hv_out[:, DH * i : DH * i + DH] = rows[8 + i : 9 + i].astype(BF16)


def body(
    queries, key_rows, value_rows, out_grad, padding, header_keys, header_values,
    neighbours, slot_valid, crystal_ids, header_index,
):
    grad = jax.ShapeDtypeStruct((BLK, 2048), BF16)
    vmem = pl.BlockSpec(memory_space=pltpu.VMEM)
    hbm = pl.BlockSpec(memory_space=pl.ANY)
    dma = pltpu.SemaphoreType.DMA
    q_grad, k_grad, v_grad, h_grad = pl.pallas_call(
        kernel,
        out_shape=(grad, grad, grad, jax.ShapeDtypeStruct((16, DH), BF16)),
        in_specs=[hbm] * 4 + [vmem] * 3 + [pl.BlockSpec(memory_space=pltpu.SMEM)] * 4,
        out_specs=[vmem] * 4,
        scratch_shapes=[
            pltpu.VMEM((HD, 4, 4, BLK, DH), BF16),
            pltpu.VMEM((10, 4, BLK, DH), BF16),
            pltpu.VMEM((10, 4, BLK, DH), BF16),
            pltpu.VMEM((10, 4, BLK, DH), BF16),
            pltpu.VMEM((2, 2, ROWS, DH), BF16),
            pltpu.VMEM((2, 2, KEYS, DH), BF16),
            pltpu.VMEM((2, KEYS, ROWS), BF16),
            pltpu.VMEM((2, KEYS, ROWS), BF16),
            pltpu.VMEM((2, KEYS, BLK), F32),
            pltpu.VMEM((2, HD, 3, MOST, BLK, DH), BF16),
            pltpu.VMEM((10, 3, BLK, DH), BF16),
            pltpu.VMEM((10, 3, BLK, DH), BF16),
            pltpu.VMEM((10, 3, BLK, DH), BF16),
            pltpu.VMEM((HD, 4, 3, BLK, DH), BF16),
            pltpu.VMEM((3, BLK, 2048), BF16),
            pltpu.VMEM((6, 8, BLK), jnp.int32),
            pltpu.SMEM((6, 8, BLK), jnp.int32),
            pltpu.VMEM((12, 8, BLK), F32),
            pltpu.VMEM((8, 16, DH), BF16),
            pltpu.VMEM((SEQ // 2, 16, DH), BF16),
            pltpu.VMEM((4, 8, DH), F32),
            pltpu.VMEM((4, 8, DH), F32),
            pltpu.VMEM((8, 48, DH), BF16),
            pltpu.VMEM((4, 8 * 48, DH), BF16),
            pltpu.VMEM((8, 8, DH), F32),
            pltpu.VMEM((8, 8, DH), F32),
            dma((HD, 4)),
            dma((HD, 4)),
            dma((HD, 4)),
            dma((10,)),
            dma((10,)),
            dma((10,)),
            dma((10,)),
            dma((HD, 3)),
            dma((HD, 3)),
            dma((HD,)),
            dma((5,)),
            dma((6,)),
            dma,
            dma((17,)),
            dma((17,)),
            dma((17,)),
            dma((17,)),
        ],
        compiler_params=pltpu.CompilerParams(
            collective_id=0, has_side_effects=True, vmem_limit_bytes=56 * 1024 * 1024
        ),
    )(*[each.reshape(2, BLK, 1024) for each in (queries, out_grad, key_rows, value_rows)], padding.reshape(2, BLK), header_keys, header_values,
      neighbours, slot_valid, crystal_ids, header_index.T)
    line = jax.ShapeDtypeStruct((1, 1024), BF16)
    return pl.pallas_call(
        finish,
        out_shape=(grad, grad, grad, line, line),
        compiler_params=pltpu.CompilerParams(vmem_limit_bytes=56 * 1024 * 1024),
    )(q_grad, k_grad, v_grad, h_grad)


def solution(mesh):
    in_specs = (
        P("seq", "head"),
        P("seq", "head"),
        P("seq", "head"),
        P("seq", "head"),
        P("seq"),
        P("seq", "head"),
        P("seq", "head"),
        P("seq", None),
        P("seq", None),
        P("seq"),
        P(),
    )
    out_specs = (
        P(("seq", "head"), None),
        P(("seq", "head"), None),
        P(("seq", "head"), None),
        P("seq", "head"),
        P("seq", "head"),
    )
    return jax.shard_map(body, mesh=mesh, in_specs=in_specs, out_specs=out_specs, check_vma=False)
```

```python
import math

import jax
import jax.numpy as jnp
from jax import lax
from jax.experimental import pallas as pl
from jax.experimental.pallas import tpu as pltpu
from jax.sharding import PartitionSpec as P

DH = 128
BLK = 128
NEG = -1e30
FACTOR = 1.0 / math.sqrt(DH)
F32 = jnp.float32
BF16 = jnp.bfloat16
HD = 4
MOST = 5
ROWS = MOST * BLK
KEYS = ROWS + 16
SEQ = 256
CAP = (6, 4)
CHUNKS = ((0, 384), (384, 640))


def kernel(
    q_in, g_in, k_in, v_in, pad_in, hk_in, hv_in, lists, valid, ids, hidx,
    q_out, k_out, v_out, h_out,
    wk, sbuf, land, imp, cqg, ckv, probs, mixes, bias, gr, rsend, rland, rw, ost, back,
    meta, meta_s, padw, tabf, table, hb, hd, hz, hx, hs, ry,
    e_send, e_recv, own_sem, f_send, f_recv, r_send, r_recv, x_send, x_recv, xown_sem,
    edge_send, edge_recv, m_send, m_recv, ms_sem, hs_send, hs_recv, ht_send, ht_recv,
):
    e = lax.axis_index("seq")
    h = lax.axis_index("head")
    core = lax.rem(e, 2)
    chip = e // 2
    j8 = lax.rem(e, 8)
    x4 = lax.rem(e // 8, 4)
    z8 = e // 32

    def wrap(index):
        return lax.rem(index + SEQ, SEQ)

    step = 2 * core - 1
    peer = e + 1 - 2 * core
    sends_to = (wrap(e + 2 * step), wrap(e - 2 * step))
    comes_from = (sends_to[1], sends_to[0])
    left, right = wrap(2 * chip - 2), wrap(2 * chip + 2)

    def y_peer(d):
        return e - j8 + lax.rem(j8 + d, 8)

    def x_peer(d):
        return e - 8 * x4 + 8 * lax.rem(x4 + d, 4)

    def z_peer(d):
        return e - 32 * z8 + 32 * lax.rem(z8 + d, 8)

    barrier = pltpu.get_barrier_semaphore()

    def greet(device, other):
        pl.semaphore_signal(barrier, inc=1, device_id=(device, other), device_id_type=pl.DeviceIdType.MESH)

    for d in range(1, 8):
        greet(y_peer(d), h)
        greet(z_peer(d), h)
    for d in range(1, 4):
        greet(x_peer(d), h)
    for c in range(2):
        greet(left + c, h)
        greet(right + c, h)
    greet(e, 1 - h)
    greet(peer, 1 - h)

    def remote(src, dst, send, recv, device, other):
        return pltpu.make_async_remote_copy(
            src_ref=src, dst_ref=dst, send_sem=send, recv_sem=recv,
            device_id=(device, other), device_id_type=pl.DeviceIdType.MESH,
        )

    ins = (q_in, g_in, k_in, v_in)

    def own_copy(array, head):
        cols = pl.ds(pl.multiple_of((core * HD + head) * DH, DH), DH)
        there = wk.at[head, array, pl.ds(2 * core, 2)]
        return pltpu.make_async_copy(ins[array].at[:, :, cols], there, own_sem.at[head, array])

    def peer_copy(array, head):
        cols = pl.ds(pl.multiple_of(((1 - core) * HD + head) * DH, DH), DH)
        there = wk.at[head, array, pl.ds(2 * core, 2)]
        return remote(ins[array].at[:, :, cols], there, e_send.at[head, array], e_recv.at[head, array], peer, h)

    for array in range(4):
        for head in range(HD):
            own_copy(array, head).start()
    lines = [each[:, DH * i : DH * i + DH] for each in (hk_in, hv_in) for i in range(8)]
    tabf[pl.ds(j8, 1)] = jnp.concatenate([line.astype(F32) for line in lines], axis=0).astype(BF16)[None]
    starts, sizes = [], []
    for block in range(2):
        first, size = jnp.int32(1 << 20), jnp.int32(0)
        for slot in range(MOST):
            used = valid[block, slot] > 0
            first = jnp.where(used, jnp.minimum(first, lists[block, slot]), first)
            size = size + jnp.where(used, 1, 0)
        starts.append(first)
        sizes.append(size)
    lines = [jnp.full((1, BLK), each, jnp.int32) for each in starts + sizes + [ids[0], ids[1]]]
    meta[pl.ds(2 + core, 1)] = jnp.concatenate([pad_in[...]] + lines, axis=0)[None]

    pl.semaphore_wait(barrier, 23)

    def edge_copy(array):
        cols = pl.ds(pl.multiple_of((core * HD + core * (HD - 1)) * DH, DH), DH)
        src = ins[array].at[core, :, cols]
        return remote(src, land.at[0, array], edge_send.at[array], edge_recv.at[array], sends_to[0], h)

    meta_to = ((peer, 2 + core), (left, 4 + core), (left + 1, 4 + core), (right, core), (right + 1, core))

    def meta_copy(kind):
        device, slot = meta_to[kind]
        return remote(meta.at[2 + core], meta.at[slot], m_send.at[kind], m_recv.at[slot], device, h)

    def meta_arrival(slot):
        return remote(meta.at[2 + core], meta.at[slot], m_send.at[0], m_recv.at[slot], peer, h)


    def row_y(d):
        return remote(tabf.at[j8], tabf.at[j8], hs_send.at[d - 1], hs_recv.at[d - 1], y_peer(d), h)

    def row_x(d):
        part = table.at[pl.ds(4 * (4 * z8 + x4), 4)]
        return remote(part, part, hs_send.at[6 + d], hs_recv.at[6 + d], x_peer(d), h)

    def row_z(d):
        part = table.at[pl.ds(16 * z8, 16)]
        return remote(part, part, hs_send.at[9 + d], hs_recv.at[9 + d], z_peer(d), h)

    for d in range(1, 8):
        row_y(d).start()
    for kind in range(5):
        meta_copy(kind).start()
    for array in range(4):
        edge_copy(array).start()
    for array in range(4):
        for head in range(HD):
            peer_copy(array, head).start()

    for slot in (0, 1, 4, 5):
        meta_arrival(slot).wait_recv()
    meta_arrival(3 - core).wait_recv()
    to_scalar = pltpu.make_async_copy(meta, meta_s, ms_sem)
    to_scalar.start()
    for d in range(1, 8):
        row_y(d).wait_recv()
    rows = tabf[...].astype(F32)
    halves = [
        jnp.concatenate([rows[:, HD * c : HD * c + HD], rows[:, 8 + HD * c : 8 + HD * c + HD]], axis=1)
        for c in range(2)
    ]
    rows = jnp.where(core == 0, halves[0], halves[1])
    table[pl.ds(4 * (4 * z8 + x4), 4)] = rows.reshape(4, 16, DH).astype(BF16)
    for d in range(1, 4):
        row_x(d).start()
    for d in range(1, 4):
        row_x(d).wait_recv()
    for d in range(1, 8):
        row_z(d).start()
    to_scalar.wait()
    start_x, size_x, id_x = meta_s[2, 2, 0] - 4 * chip, meta_s[2, 4, 0], meta_s[2, 6, 0]
    start_y, size_y, id_y = meta_s[3, 3, 0] - 4 * chip, meta_s[3, 5, 0], meta_s[3, 7, 0]
    a_x = jnp.maximum(-start_x, 0)
    b_x = size_x - a_x
    b_y = jnp.maximum(start_y + size_y - 4, 0)
    a_y = size_y - b_y
    cross_x, cross_y = a_x > 0, b_y > 0
    same = id_x == id_y
    on_x = jnp.logical_not(same & cross_y)
    on_y = jnp.logical_not(same) | cross_y

    def left_heads(a, b):
        return jnp.where(b == 1, 3, jnp.where(a == 1, 1, jnp.where(b == 2, 3 - core, 2 - core)))

    split_x, split_y = left_heads(a_x, b_x), left_heads(a_y, b_y)

    def home_x(head):
        return jnp.logical_not(cross_x) | (head >= split_x)

    def home_y(head):
        return jnp.logical_not(cross_y) | (head < split_y)

    is_x = (core == 1, core == 0)

    def pick(unit, of_x, of_y):
        return jnp.where(is_x[unit], of_x, of_y)

    start_u = [pick(u, start_x, start_y) for u in range(2)]
    size_u = [pick(u, size_x, size_y) for u in range(2)]
    width_u = [pick(u, a_x, b_y) for u in range(2)]
    given_u = [pick(u, b_x, a_y) for u in range(2)]
    id_u = [pick(u, id_x, id_y) for u in range(2)]
    on_u = [pick(u, on_x, on_y) for u in range(2)]

    def over(slot, width):
        by = [slot // n for n in range(1, 5)]
        return jnp.where(width == 2, by[1], jnp.where(width == 3, by[2], jnp.where(width == 4, by[3], by[0])))

    def rest(slot, width):
        return slot - over(slot, width) * jnp.clip(width, 1, 4)

    for array in range(4):
        for head in range(HD):
            own_copy(array, head).wait()
            peer_copy(array, head).wait_recv()

    def forward(d, slot):
        at = 6 * d + slot
        return remote(sbuf.at[at], land.at[at], f_send.at[at], f_recv.at[at], sends_to[d], h)

    def send(d, slot):
        unit = 1 - d
        width = given_u[unit]
        order = jnp.clip(over(slot, width), 0, HD - 1)
        part = rest(slot, width)
        head = pick(unit, order, HD - 1 - order)
        block = jnp.clip(pick(unit, part, 3 - part), 0, 3)
        sbuf[6 * d + slot] = wk[head, :, block]
        forward(d, slot).start()

    for slot in range(1, 6):
        send(0, slot)
    for slot in range(4):
        send(1, slot)

    for slot in range(6):
        for block in range(2):
            padw[2 * slot + block] = jnp.broadcast_to(meta[slot, block : block + 1, :].astype(F32), (8, BLK))
    for u in range(2):
        for p in range(MOST):
            line = padw[jnp.clip(start_u[u] + p + 4, 0, 11)][0:1]
            full = jnp.broadcast_to(line, (BLK, BLK)).T
            full = jnp.where(p < size_u[u], full, 0.0)
            bias[u, p * BLK : p * BLK + BLK, :] = jnp.where(full > 0.0, 0.0, NEG)
        at = lax.broadcasted_iota(jnp.int32, (16, BLK), 0)
        bias[u, ROWS:KEYS, :] = jnp.where(at < 2, 0.0, NEG)

    for d in range(1, 8):
        row_z(d).wait_recv()
    names = []
    for u in range(2):
        for slot in range(2):
            row = hidx[slot, id_u[u]]
            pair = table[lax.div(row, 2)].astype(F32)
            hb[2 * u + slot] = jnp.where(lax.rem(row, 2) == 0, pair[0:8], pair[8:16])
            names.append(jnp.where(on_u[u], row, -1))

    def nt(a, b):
        return lax.dot_general(a, b, (((1,), (1,)), ((), ())), preferred_element_type=F32)

    def give_back(d, slot):
        at = 6 * d + slot
        return remote(rsend.at[at], rland.at[at], r_send.at[at], r_recv.at[at], comes_from[d], h)

    def send_back(d, slot):
        part = rest(slot, width_u[d])
        turn = jnp.clip(over(slot, width_u[d]), 0, HD - 1)
        p = jnp.clip(pick(d, a_x - 1 - part, part + 4 - start_u[d]), 0, MOST - 1)
        rsend[6 * d + slot] = gr[d, turn, :, p]
        give_back(d, slot).start()

    def work(n, carry):
        late = n // 6
        u = (1 - late) * (n // 3) + late * (n - 6)
        turn = (1 - late) * lax.rem(n, 3) + late * 3

        @pl.when(n == 0)
        def _():
            for array in range(4):
                edge_copy(array).wait_recv()
            imp[0] = land[0]
            for slot in range(1, 4):
                forward(0, slot).wait_recv()
                imp[slot] = land[slot]

        @pl.when(n == 1)
        def _():
            for slot in range(4, 6):
                forward(0, slot).wait_recv()
                imp[slot] = land[slot]

        @pl.when(n == 3)
        def _():
            for slot in range(4):
                forward(1, slot).wait_recv()
                imp[6 + slot] = land[6 + slot]

        wide = u == 0
        start = jnp.where(wide, start_u[0], start_u[1])
        size = jnp.where(wide, size_u[0], size_u[1])
        width = jnp.where(wide, width_u[0], width_u[1])
        first = core + u * (1 - 2 * core) == 1
        head = turn + (core + u * (1 - 2 * core)) * (HD - 1 - 2 * turn)
        last = jnp.where((n == 0) | (u == 1), 3, CAP[0] - 1)
        for p in range(MOST):
            there = start + p
            slot = turn * width + jnp.where(first, -1 - there, there - 4)
            outside = (there < 0) | (there > 3)
            far = imp[6 * u + jnp.clip(slot, 0, last)]
            near = wk[head, :, jnp.clip(there, 0, 3)]
            rows = jnp.where(outside, far, near)
            span = slice(p * BLK, p * BLK + BLK)
            cqg[u, :, span, :] = jnp.where(p < size, rows[0:2], jnp.zeros_like(rows[0:2]))
            ckv[u, :, span, :] = rows[2:4]
        for array in range(2):
            at = pl.ds(array * HD + head, 1)
            lines = [hb[2 * u + slot, at, :] for slot in range(2)] + [jnp.zeros((14, DH), F32)]
            ckv[u, array, ROWS:KEYS, :] = jnp.concatenate(lines, axis=0).astype(BF16)
        for lo, hi in CHUNKS:
            q = cqg[u, 0, lo:hi, :]
            g = cqg[u, 1, lo:hi, :]
            keys = ckv[u, 0]
            values = ckv[u, 1]
            mask = bias[u]
            mask = jnp.concatenate([mask] * ((hi - lo) // BLK), axis=1)
            score = nt(keys, q) * FACTOR + mask
            top = jnp.max(score, axis=0, keepdims=True)
            grown = jnp.exp(score - top)
            prob = grown * (1.0 / jnp.sum(grown, axis=0, keepdims=True))
            low = prob.astype(BF16)
            dprob = nt(values, g)
            delta = jnp.sum(low.astype(F32) * dprob, axis=0, keepdims=True)
            mixing = (FACTOR * prob * (dprob - delta)).astype(BF16)
            probs[u, :, lo:hi] = low
            mixes[u, :, lo:hi] = mixing
            q_grad = lax.dot_general(mixing, keys, (((0,), (0,)), ((), ())), preferred_element_type=F32)
            gr[u, turn, 0, lo // BLK : hi // BLK] = q_grad.astype(BF16).reshape(-1, BLK, DH)
        here = jnp.where(first, home_x(head).astype(jnp.int32), home_y(head).astype(jnp.int32)) > 0
        for array, weights in ((0, mixes), (1, probs)):
            total = jnp.dot(weights[u], cqg[u, array], preferred_element_type=F32)
            gr[u, turn, 1 + array] = total[0:ROWS].astype(BF16).reshape(MOST, BLK, DH)
            for slot in range(2):
                line = total[ROWS + slot : ROWS + slot + 1]
                hd[2 * u + slot, pl.ds(array * HD + head, 1), :] = jnp.where(here, line, 0.0)

        for after, slots in enumerate(((0,), (1, 3), (2, 4, 5))):
            for d in range(2):

                @pl.when(n == after + 3 * d)
                def _(d=d, slots=slots):
                    for slot in slots:
                        if slot < CAP[d]:
                            send_back(d, slot)

        return carry

    lax.fori_loop(0, 2 * HD, work, 0)

    tags = [jnp.full((1, DH), name).astype(F32) for name in names] + [jnp.full((12, DH), -1.0, F32)]
    block = jnp.concatenate([hd[slot] for slot in range(4)] + tags, axis=0)
    hz[pl.ds(z8, 1)] = block.astype(BF16)[None]

    def out_z(d):
        return remote(hz.at[z8], hz.at[z8], ht_send.at[d - 1], ht_recv.at[d - 1], z_peer(d), h)

    def out_x(d):
        return remote(hx.at[x4], hx.at[x4], ht_send.at[6 + d], ht_recv.at[6 + d], x_peer(d), h)

    def out_y(d):
        src = hs.at[lax.rem(j8 + d, 8)]
        return remote(src, ry.at[j8], ht_send.at[9 + d], ht_recv.at[9 + d], y_peer(d), h)

    for d in range(1, 8):
        out_z(d).start()

    mine = 2 * core + h

    def column(head):
        return pl.ds(pl.multiple_of(h * 1024 + (core * HD + head) * DH, DH), DH)

    def deliver(d, head):
        there = lax.rem(mine + d, 4)
        return remote(
            ost.at[head, there], back.at[:, :, column(head)], x_send.at[head, d - 1], x_recv.at[head, d - 1],
            2 * chip + there // 2, lax.rem(there, 2),
        )

    def keep(head):
        return pltpu.make_async_copy(ost.at[head, mine], back.at[:, :, column(head)], xown_sem.at[head])

    for slot in range(4):
        for d in range(2):
            give_back(d, slot).wait_recv()
            rw[6 * d + slot] = rland[6 * d + slot]
    unit_x = jnp.where(core == 1, 0, 1)

    def assemble(head, carry):
        for j in range(4):
            in_x = on_x & (j < start_x + size_x)
            unit = jnp.where(in_x, unit_x, 1 - unit_x)
            when = jnp.where(in_x, HD - 1 - head, head)
            p = jnp.clip(jnp.where(in_x, j - start_x, j - start_y), 0, MOST - 1)
            slot = jnp.where(in_x, head * b_x + j, (HD - 1 - head) * a_y + 3 - j)
            here = jnp.where(in_x, home_x(head).astype(jnp.int32), home_y(head).astype(jnp.int32)) > 0
            most = jnp.where(unit == 1, CAP[0] - 1, CAP[1] - 1)
            at = 6 * (1 - unit) + jnp.clip(slot, 0, most)
            worked = gr[unit, when, :, p]
            ost[head, j] = jnp.where(here, worked, rw[at])
        for d in range(1, 4):
            deliver(d, head).start()
        keep(head).start()
        return carry

    def assemble_pair(one, two):
        lax.fori_loop(0, 2, lambda i, carry: assemble(one + (two - one) * i, carry), 0)

    assemble_pair(0, 3)
    for slot in range(4, 6):
        give_back(0, slot).wait_recv()
        rw[slot] = rland[slot]
    assemble_pair(1, 2)

    for d in range(1, 8):
        out_z(d).wait_recv()
    hx[pl.ds(x4, 1)] = hz[...].reshape(1, 8 * 48, DH)
    for d in range(1, 4):
        out_x(d).start()
    for d in range(1, 4):
        out_x(d).wait_recv()
    first = 32 * z8 + 8 * x4

    def gather(at, totals):
        block = hx[at // 8, pl.ds(pl.multiple_of(lax.rem(at, 8) * 48, 16), 48), :].astype(F32)
        totals = list(totals)
        for slot in range(4):
            tag = jnp.broadcast_to(block[32 + slot : 33 + slot], (8, DH)) - first.astype(F32)
            for j in range(8):
                totals[j] = totals[j] + jnp.where(tag == float(j), block[8 * slot : 8 * slot + 8], 0.0)
        return tuple(totals)

    totals = lax.fori_loop(0, 32, gather, tuple(jnp.zeros((8, DH), F32) for _ in range(8)))
    for j in range(8):
        hs[j] = totals[j]
    for d in range(1, 8):
        out_y(d).start()
    ry[pl.ds(j8, 1)] = hs[pl.ds(j8, 1)]
    for d in range(1, 8):
        out_y(d).wait_recv()
    halves = [ry[c] + ry[c + 2] + ry[c + 4] + ry[c + 6] for c in range(2)]
    lines = [halves[0][0:4], halves[1][0:4], halves[0][4:8], halves[1][4:8]]
    h_out[...] = jnp.concatenate(lines, axis=0).astype(BF16)

    def settle(head, carry):
        for d in range(1, 4):
            deliver(d, head).wait_recv()
        keep(head).wait()
        return carry

    lax.fori_loop(0, HD, settle, 0)
    for array, out in ((0, q_out), (1, k_out), (2, v_out)):
        out[...] = back[array]

    for array in range(4):
        for head in range(HD):
            peer_copy(array, head).wait_send()
    for d in range(2):
        for slot in range(CAP[d]):
            if d + slot > 0:
                forward(d, slot).wait_send()
            give_back(d, slot).wait_send()
    for array in range(4):
        edge_copy(array).wait_send()
    for head in range(HD):
        for d in range(1, 4):
            deliver(d, head).wait_send()
    for kind in range(5):
        meta_copy(kind).wait_send()
    for d in range(1, 8):
        row_y(d).wait_send()
        row_z(d).wait_send()
        out_y(d).wait_send()
        out_z(d).wait_send()
    for d in range(1, 4):
        row_x(d).wait_send()
        out_x(d).wait_send()


def finish(q_in, k_in, v_in, h_in, q_out, k_out, v_out, hk_out, hv_out):
    q_out[...] = q_in[...]
    k_out[...] = k_in[...]
    v_out[...] = v_in[...]
    rows = h_in[...].astype(F32)
    for i in range(8):
        hk_out[:, DH * i : DH * i + DH] = rows[i : i + 1].astype(BF16)
        hv_out[:, DH * i : DH * i + DH] = rows[8 + i : 9 + i].astype(BF16)


def body(
    queries, key_rows, value_rows, out_grad, padding, header_keys, header_values,
    neighbours, slot_valid, crystal_ids, header_index,
):
    grad = jax.ShapeDtypeStruct((BLK, 2048), BF16)
    vmem = pl.BlockSpec(memory_space=pltpu.VMEM)
    hbm = pl.BlockSpec(memory_space=pl.ANY)
    dma = pltpu.SemaphoreType.DMA
    q_grad, k_grad, v_grad, h_grad = pl.pallas_call(
        kernel,
        out_shape=(grad, grad, grad, jax.ShapeDtypeStruct((16, DH), BF16)),
        in_specs=[hbm] * 4 + [vmem] * 3 + [pl.BlockSpec(memory_space=pltpu.SMEM)] * 4,
        out_specs=[vmem] * 4,
        scratch_shapes=[
            pltpu.VMEM((HD, 4, 4, BLK, DH), BF16),
            pltpu.VMEM((10, 4, BLK, DH), BF16),
            pltpu.VMEM((10, 4, BLK, DH), BF16),
            pltpu.VMEM((10, 4, BLK, DH), BF16),
            pltpu.VMEM((2, 2, ROWS, DH), BF16),
            pltpu.VMEM((2, 2, KEYS, DH), BF16),
            pltpu.VMEM((2, KEYS, ROWS), BF16),
            pltpu.VMEM((2, KEYS, ROWS), BF16),
            pltpu.VMEM((2, KEYS, BLK), F32),
            pltpu.VMEM((2, HD, 3, MOST, BLK, DH), BF16),
            pltpu.VMEM((10, 3, BLK, DH), BF16),
            pltpu.VMEM((10, 3, BLK, DH), BF16),
            pltpu.VMEM((10, 3, BLK, DH), BF16),
            pltpu.VMEM((HD, 4, 3, BLK, DH), BF16),
            pltpu.VMEM((3, BLK, 2048), BF16),
            pltpu.VMEM((6, 8, BLK), jnp.int32),
            pltpu.SMEM((6, 8, BLK), jnp.int32),
            pltpu.VMEM((12, 8, BLK), F32),
            pltpu.VMEM((8, 16, DH), BF16),
            pltpu.VMEM((SEQ // 2, 16, DH), BF16),
            pltpu.VMEM((4, 8, DH), F32),
            pltpu.VMEM((4, 8, DH), F32),
            pltpu.VMEM((8, 48, DH), BF16),
            pltpu.VMEM((4, 8 * 48, DH), BF16),
            pltpu.VMEM((8, 8, DH), F32),
            pltpu.VMEM((8, 8, DH), F32),
            dma((HD, 4)),
            dma((HD, 4)),
            dma((HD, 4)),
            dma((10,)),
            dma((10,)),
            dma((10,)),
            dma((10,)),
            dma((HD, 3)),
            dma((HD, 3)),
            dma((HD,)),
            dma((4,)),
            dma((4,)),
            dma((5,)),
            dma((6,)),
            dma,
            dma((17,)),
            dma((17,)),
            dma((17,)),
            dma((17,)),
        ],
        compiler_params=pltpu.CompilerParams(
            collective_id=0, has_side_effects=True, vmem_limit_bytes=56 * 1024 * 1024
        ),
    )(*[each.reshape(2, BLK, 1024) for each in (queries, out_grad, key_rows, value_rows)], padding.reshape(2, BLK), header_keys, header_values,
      neighbours, slot_valid, crystal_ids, header_index.T)
    line = jax.ShapeDtypeStruct((1, 1024), BF16)
    return pl.pallas_call(
        finish,
        out_shape=(grad, grad, grad, line, line),
        compiler_params=pltpu.CompilerParams(vmem_limit_bytes=56 * 1024 * 1024),
    )(q_grad, k_grad, v_grad, h_grad)


def solution(mesh):
    in_specs = (
        P("seq", "head"),
        P("seq", "head"),
        P("seq", "head"),
        P("seq", "head"),
        P("seq"),
        P("seq", "head"),
        P("seq", "head"),
        P("seq", None),
        P("seq", None),
        P("seq"),
        P(),
    )
    out_specs = (
        P(("seq", "head"), None),
        P(("seq", "head"), None),
        P(("seq", "head"), None),
        P("seq", "head"),
        P("seq", "head"),
    )
    return jax.shard_map(body, mesh=mesh, in_specs=in_specs, out_specs=out_specs, check_vma=False)
```

```python
import math

import jax
import jax.numpy as jnp
from jax import lax
from jax.experimental import pallas as pl
from jax.experimental.pallas import tpu as pltpu
from jax.sharding import PartitionSpec as P

DH = 128
BLK = 128
NEG = -1e30
FACTOR = 1.0 / math.sqrt(DH)
F32 = jnp.float32
BF16 = jnp.bfloat16
HD = 4
MOST = 5
ROWS = MOST * BLK
KEYS = ROWS + 16
SEQ = 256
CAP = (6, 4)
CHUNKS = ((0, 384), (384, 640))


def kernel(
    q_in, g_in, k_in, v_in, pad_in, hk_in, hv_in, lists, valid, ids, hidx,
    q_out, k_out, v_out, h_out,
    wk, sbuf, land, imp, cqg, ckv, probs, mixes, bias, gr, rsend, rland, rw, ost, back,
    meta, meta_s, padw, tabf, table, hb, hd, hz, hx, hs, ry,
    e_send, e_recv, own_sem, f_send, f_recv, r_send, r_recv, x_send, x_recv, xown_sem,
    edge_send, edge_recv, m_send, m_recv, ms_sem, hs_send, hs_recv, ht_send, ht_recv,
):
    e = lax.axis_index("seq")
    h = lax.axis_index("head")
    core = lax.rem(e, 2)
    chip = e // 2
    j8 = lax.rem(e, 8)
    x4 = lax.rem(e // 8, 4)
    z8 = e // 32

    def wrap(index):
        return lax.rem(index + SEQ, SEQ)

    step = 2 * core - 1
    peer = e + 1 - 2 * core
    sends_to = (wrap(e + 2 * step), wrap(e - 2 * step))
    comes_from = (sends_to[1], sends_to[0])
    left, right = wrap(2 * chip - 2), wrap(2 * chip + 2)

    def y_peer(d):
        return e - j8 + lax.rem(j8 + d, 8)

    def x_peer(d):
        return e - 8 * x4 + 8 * lax.rem(x4 + d, 4)

    def z_peer(d):
        return e - 32 * z8 + 32 * lax.rem(z8 + d, 8)

    barrier = pltpu.get_barrier_semaphore()

    def greet(device, other):
        pl.semaphore_signal(barrier, inc=1, device_id=(device, other), device_id_type=pl.DeviceIdType.MESH)

    for d in range(1, 8):
        greet(y_peer(d), h)
        greet(z_peer(d), h)
    for d in range(1, 4):
        greet(x_peer(d), h)
    for c in range(2):
        greet(left + c, h)
        greet(right + c, h)
    greet(e, 1 - h)
    greet(peer, 1 - h)

    def remote(src, dst, send, recv, device, other):
        return pltpu.make_async_remote_copy(
            src_ref=src, dst_ref=dst, send_sem=send, recv_sem=recv,
            device_id=(device, other), device_id_type=pl.DeviceIdType.MESH,
        )

    ins = (q_in, g_in, k_in, v_in)

    def own_copy(array, head):
        cols = pl.ds(pl.multiple_of((core * HD + head) * DH, DH), DH)
        there = wk.at[head, array, pl.ds(2 * core, 2)]
        return pltpu.make_async_copy(ins[array].at[:, :, cols], there, own_sem.at[head, array])

    def peer_copy(array, head):
        cols = pl.ds(pl.multiple_of(((1 - core) * HD + head) * DH, DH), DH)
        there = wk.at[head, array, pl.ds(2 * core, 2)]
        return remote(ins[array].at[:, :, cols], there, e_send.at[head, array], e_recv.at[head, array], peer, h)

    for array in range(4):
        for head in range(HD):
            own_copy(array, head).start()
    lines = [each[:, DH * i : DH * i + DH] for each in (hk_in, hv_in) for i in range(8)]
    tabf[pl.ds(j8, 1)] = jnp.concatenate([line.astype(F32) for line in lines], axis=0).astype(BF16)[None]
    starts, sizes = [], []
    for block in range(2):
        first, size = jnp.int32(1 << 20), jnp.int32(0)
        for slot in range(MOST):
            used = valid[block, slot] > 0
            first = jnp.where(used, jnp.minimum(first, lists[block, slot]), first)
            size = size + jnp.where(used, 1, 0)
        starts.append(first)
        sizes.append(size)
    lines = [jnp.full((1, BLK), each, jnp.int32) for each in starts + sizes + [ids[0], ids[1]]]
    meta[pl.ds(2 + core, 1)] = jnp.concatenate([pad_in[...]] + lines, axis=0)[None]

    pl.semaphore_wait(barrier, 23)

    def edge_copy(array):
        cols = pl.ds(pl.multiple_of((core * HD + core * (HD - 1)) * DH, DH), DH)
        src = ins[array].at[core, :, cols]
        return remote(src, land.at[0, array], edge_send.at[array], edge_recv.at[array], sends_to[0], h)

    meta_to = ((peer, 2 + core), (left, 4 + core), (left + 1, 4 + core), (right, core), (right + 1, core))

    def meta_copy(kind):
        device, slot = meta_to[kind]
        return remote(meta.at[2 + core], meta.at[slot], m_send.at[kind], m_recv.at[slot], device, h)

    def meta_arrival(slot):
        return remote(meta.at[2 + core], meta.at[slot], m_send.at[0], m_recv.at[slot], peer, h)


    def row_y(d):
        return remote(tabf.at[j8], tabf.at[j8], hs_send.at[d - 1], hs_recv.at[d - 1], y_peer(d), h)

    def row_x(d):
        part = table.at[pl.ds(4 * (4 * z8 + x4), 4)]
        return remote(part, part, hs_send.at[6 + d], hs_recv.at[6 + d], x_peer(d), h)

    def row_z(d):
        part = table.at[pl.ds(16 * z8, 16)]
        return remote(part, part, hs_send.at[9 + d], hs_recv.at[9 + d], z_peer(d), h)

    for d in range(1, 8):
        row_y(d).start()
    for kind in range(5):
        meta_copy(kind).start()
    for array in range(4):
        edge_copy(array).start()
    for array in range(4):
        for head in range(HD):
            peer_copy(array, head).start()

    for slot in (0, 1, 4, 5):
        meta_arrival(slot).wait_recv()
    meta_arrival(3 - core).wait_recv()
    to_scalar = pltpu.make_async_copy(meta, meta_s, ms_sem)
    to_scalar.start()
    for d in range(1, 8):
        row_y(d).wait_recv()
    rows = tabf[...].astype(F32)
    halves = [
        jnp.concatenate([rows[:, HD * c : HD * c + HD], rows[:, 8 + HD * c : 8 + HD * c + HD]], axis=1)
        for c in range(2)
    ]
    rows = jnp.where(core == 0, halves[0], halves[1])
    table[pl.ds(4 * (4 * z8 + x4), 4)] = rows.reshape(4, 16, DH).astype(BF16)
    for d in range(1, 4):
        row_x(d).start()
    for d in range(1, 4):
        row_x(d).wait_recv()
    for d in range(1, 8):
        row_z(d).start()
    to_scalar.wait()
    start_x, size_x, id_x = meta_s[2, 2, 0] - 4 * chip, meta_s[2, 4, 0], meta_s[2, 6, 0]
    start_y, size_y, id_y = meta_s[3, 3, 0] - 4 * chip, meta_s[3, 5, 0], meta_s[3, 7, 0]
    a_x = jnp.maximum(-start_x, 0)
    b_x = size_x - a_x
    b_y = jnp.maximum(start_y + size_y - 4, 0)
    a_y = size_y - b_y
    cross_x, cross_y = a_x > 0, b_y > 0
    same = id_x == id_y
    on_x = jnp.logical_not(same & cross_y)
    on_y = jnp.logical_not(same) | cross_y

    def left_heads(a, b):
        return jnp.where(b == 1, 3, jnp.where(a == 1, 1, jnp.where(b == 2, 3 - core, 2 - core)))

    split_x, split_y = left_heads(a_x, b_x), left_heads(a_y, b_y)

    def home_x(head):
        return jnp.logical_not(cross_x) | (head >= split_x)

    def home_y(head):
        return jnp.logical_not(cross_y) | (head < split_y)

    is_x = (core == 1, core == 0)

    def pick(unit, of_x, of_y):
        return jnp.where(is_x[unit], of_x, of_y)

    start_u = [pick(u, start_x, start_y) for u in range(2)]
    size_u = [pick(u, size_x, size_y) for u in range(2)]
    width_u = [pick(u, a_x, b_y) for u in range(2)]
    given_u = [pick(u, b_x, a_y) for u in range(2)]
    id_u = [pick(u, id_x, id_y) for u in range(2)]
    on_u = [pick(u, on_x, on_y) for u in range(2)]

    def over(slot, width):
        by = [slot // n for n in range(1, 5)]
        return jnp.where(width == 2, by[1], jnp.where(width == 3, by[2], jnp.where(width == 4, by[3], by[0])))

    def rest(slot, width):
        return slot - over(slot, width) * jnp.clip(width, 1, 4)

    for array in range(4):
        for head in range(HD):
            own_copy(array, head).wait()
            peer_copy(array, head).wait_recv()

    def forward(d, slot):
        at = 6 * d + slot
        return remote(sbuf.at[at], land.at[at], f_send.at[at], f_recv.at[at], sends_to[d], h)

    def send(d, slot):
        unit = 1 - d
        width = given_u[unit]
        order = jnp.clip(over(slot, width), 0, HD - 1)
        part = rest(slot, width)
        head = pick(unit, order, HD - 1 - order)
        block = jnp.clip(pick(unit, part, 3 - part), 0, 3)
        sbuf[6 * d + slot] = wk[head, :, block]
        forward(d, slot).start()

    for slot in range(1, 6):
        send(0, slot)
    for slot in range(4):
        send(1, slot)

    for slot in range(6):
        for block in range(2):
            padw[2 * slot + block] = jnp.broadcast_to(meta[slot, block : block + 1, :].astype(F32), (8, BLK))
    for u in range(2):
        for p in range(MOST):
            line = padw[jnp.clip(start_u[u] + p + 4, 0, 11)][0:1]
            full = jnp.broadcast_to(line, (BLK, BLK)).T
            full = jnp.where(p < size_u[u], full, 0.0)
            bias[u, p * BLK : p * BLK + BLK, :] = jnp.where(full > 0.0, 0.0, NEG)
        at = lax.broadcasted_iota(jnp.int32, (16, BLK), 0)
        bias[u, ROWS:KEYS, :] = jnp.where(at < 2, 0.0, NEG)

    for d in range(1, 8):
        row_z(d).wait_recv()
    names = []
    for u in range(2):
        for slot in range(2):
            row = hidx[slot, id_u[u]]
            pair = table[lax.div(row, 2)].astype(F32)
            hb[2 * u + slot] = jnp.where(lax.rem(row, 2) == 0, pair[0:8], pair[8:16])
            names.append(jnp.where(on_u[u], row, -1))

    def nt(a, b):
        return lax.dot_general(a, b, (((1,), (1,)), ((), ())), preferred_element_type=F32)

    def give_back(d, slot):
        at = 6 * d + slot
        return remote(rsend.at[at], rland.at[at], r_send.at[at], r_recv.at[at], comes_from[d], h)

    def send_back(d, slot):
        part = rest(slot, width_u[d])
        turn = jnp.clip(over(slot, width_u[d]), 0, HD - 1)
        p = jnp.clip(pick(d, a_x - 1 - part, part + 4 - start_u[d]), 0, MOST - 1)
        rsend[6 * d + slot] = gr[d, turn, :, p]
        give_back(d, slot).start()

    def work(n, carry):
        late = n // 6
        u = (1 - late) * (n // 3) + late * (n - 6)
        turn = (1 - late) * lax.rem(n, 3) + late * 3

        @pl.when(n == 0)
        def _():
            for array in range(4):
                edge_copy(array).wait_recv()
            imp[0] = land[0]
            for slot in range(1, 4):
                forward(0, slot).wait_recv()
                imp[slot] = land[slot]

        @pl.when(n == 1)
        def _():
            for slot in range(4, 6):
                forward(0, slot).wait_recv()
                imp[slot] = land[slot]

        @pl.when(n == 3)
        def _():
            for slot in range(4):
                forward(1, slot).wait_recv()
                imp[6 + slot] = land[6 + slot]

        wide = u == 0
        start = jnp.where(wide, start_u[0], start_u[1])
        size = jnp.where(wide, size_u[0], size_u[1])
        width = jnp.where(wide, width_u[0], width_u[1])
        first = core + u * (1 - 2 * core) == 1
        head = turn + (core + u * (1 - 2 * core)) * (HD - 1 - 2 * turn)
        last = jnp.where((n == 0) | (u == 1), 3, CAP[0] - 1)
        for p in range(MOST):
            there = start + p
            slot = turn * width + jnp.where(first, -1 - there, there - 4)
            outside = (there < 0) | (there > 3)
            far = imp[6 * u + jnp.clip(slot, 0, last)]
            near = wk[head, :, jnp.clip(there, 0, 3)]
            rows = jnp.where(outside, far, near)
            span = slice(p * BLK, p * BLK + BLK)
            cqg[u, :, span, :] = jnp.where(p < size, rows[0:2], jnp.zeros_like(rows[0:2]))
            ckv[u, :, span, :] = rows[2:4]
        for array in range(2):
            at = pl.ds(array * HD + head, 1)
            lines = [hb[2 * u + slot, at, :] for slot in range(2)] + [jnp.zeros((14, DH), F32)]
            ckv[u, array, ROWS:KEYS, :] = jnp.concatenate(lines, axis=0).astype(BF16)
        for lo, hi in CHUNKS:
            q = cqg[u, 0, lo:hi, :]
            g = cqg[u, 1, lo:hi, :]
            keys = ckv[u, 0]
            values = ckv[u, 1]
            mask = bias[u]
            mask = jnp.concatenate([mask] * ((hi - lo) // BLK), axis=1)
            score = nt(keys, q) * FACTOR + mask
            top = jnp.max(score, axis=0, keepdims=True)
            grown = jnp.exp(score - top)
            prob = grown * (1.0 / jnp.sum(grown, axis=0, keepdims=True))
            low = prob.astype(BF16)
            dprob = nt(values, g)
            delta = jnp.sum(low.astype(F32) * dprob, axis=0, keepdims=True)
            mixing = (FACTOR * prob * (dprob - delta)).astype(BF16)
            probs[u, :, lo:hi] = low
            mixes[u, :, lo:hi] = mixing
            q_grad = lax.dot_general(mixing, keys, (((0,), (0,)), ((), ())), preferred_element_type=F32)
            gr[u, turn, 0, lo // BLK : hi // BLK] = q_grad.astype(BF16).reshape(-1, BLK, DH)
        here = jnp.where(first, home_x(head).astype(jnp.int32), home_y(head).astype(jnp.int32)) > 0
        for array, weights in ((0, mixes), (1, probs)):
            total = jnp.dot(weights[u], cqg[u, array], preferred_element_type=F32)
            gr[u, turn, 1 + array] = total[0:ROWS].astype(BF16).reshape(MOST, BLK, DH)
            for slot in range(2):
                line = total[ROWS + slot : ROWS + slot + 1]
                hd[2 * u + slot, pl.ds(array * HD + head, 1), :] = jnp.where(here, line, 0.0)

        for after, slots in enumerate(((0,), (1, 3), (2, 4, 5))):
            for d in range(2):

                @pl.when(n == after + 3 * d)
                def _(d=d, slots=slots):
                    for slot in slots:
                        if slot < CAP[d]:
                            send_back(d, slot)

        return carry

    lax.fori_loop(0, 2 * HD - 1, work, 0)

    mine = 2 * core + h

    def column(head):
        return pl.ds(pl.multiple_of(h * 1024 + (core * HD + head) * DH, DH), DH)

    def deliver(d, head):
        there = lax.rem(mine + d, 4)
        return remote(
            ost.at[head, there], back.at[:, :, column(head)], x_send.at[head, d - 1], x_recv.at[head, d - 1],
            2 * chip + there // 2, lax.rem(there, 2),
        )

    def keep(head):
        return pltpu.make_async_copy(ost.at[head, mine], back.at[:, :, column(head)], xown_sem.at[head])

    for d in range(2):
        for slot in range(CAP[d]):
            give_back(d, slot).wait_recv()
            rw[6 * d + slot] = rland[6 * d + slot]
    unit_x = jnp.where(core == 1, 0, 1)

    def assemble(head, carry):
        for j in range(4):
            in_x = on_x & (j < start_x + size_x)
            unit = jnp.where(in_x, unit_x, 1 - unit_x)
            when = jnp.where(in_x, HD - 1 - head, head)
            p = jnp.clip(jnp.where(in_x, j - start_x, j - start_y), 0, MOST - 1)
            slot = jnp.where(in_x, head * b_x + j, (HD - 1 - head) * a_y + 3 - j)
            here = jnp.where(in_x, home_x(head).astype(jnp.int32), home_y(head).astype(jnp.int32)) > 0
            most = jnp.where(unit == 1, CAP[0] - 1, CAP[1] - 1)
            at = 6 * (1 - unit) + jnp.clip(slot, 0, most)
            worked = gr[unit, when, :, p]
            ost[head, j] = jnp.where(here, worked, rw[at])
        for d in range(1, 4):
            deliver(d, head).start()
        keep(head).start()
        return carry

    def assemble_pair(one, two):
        lax.fori_loop(0, 2, lambda i, carry: assemble(one + (two - one) * i, carry), 0)

    assemble_pair(1, 2)
    work(2 * HD - 1, 0)

    tags = [jnp.full((1, DH), name).astype(F32) for name in names] + [jnp.full((12, DH), -1.0, F32)]
    block = jnp.concatenate([hd[slot] for slot in range(4)] + tags, axis=0)
    hz[pl.ds(z8, 1)] = block.astype(BF16)[None]

    def out_z(d):
        return remote(hz.at[z8], hz.at[z8], ht_send.at[d - 1], ht_recv.at[d - 1], z_peer(d), h)

    def out_x(d):
        return remote(hx.at[x4], hx.at[x4], ht_send.at[6 + d], ht_recv.at[6 + d], x_peer(d), h)

    def out_y(d):
        src = hs.at[lax.rem(j8 + d, 8)]
        return remote(src, ry.at[j8], ht_send.at[9 + d], ht_recv.at[9 + d], y_peer(d), h)

    for d in range(1, 8):
        out_z(d).start()
    assemble_pair(0, 3)

    for d in range(1, 8):
        out_z(d).wait_recv()
    hx[pl.ds(x4, 1)] = hz[...].reshape(1, 8 * 48, DH)
    for d in range(1, 4):
        out_x(d).start()
    for d in range(1, 4):
        out_x(d).wait_recv()
    first = 32 * z8 + 8 * x4

    def gather(at, totals):
        block = hx[at // 8, pl.ds(pl.multiple_of(lax.rem(at, 8) * 48, 16), 48), :].astype(F32)
        totals = list(totals)
        for slot in range(4):
            tag = jnp.broadcast_to(block[32 + slot : 33 + slot], (8, DH)) - first.astype(F32)
            for j in range(8):
                totals[j] = totals[j] + jnp.where(tag == float(j), block[8 * slot : 8 * slot + 8], 0.0)
        return tuple(totals)

    totals = lax.fori_loop(0, 32, gather, tuple(jnp.zeros((8, DH), F32) for _ in range(8)))
    for j in range(8):
        hs[j] = totals[j]
    for d in range(1, 8):
        out_y(d).start()
    ry[pl.ds(j8, 1)] = hs[pl.ds(j8, 1)]
    for d in range(1, 8):
        out_y(d).wait_recv()
    halves = [ry[c] + ry[c + 2] + ry[c + 4] + ry[c + 6] for c in range(2)]
    lines = [halves[0][0:4], halves[1][0:4], halves[0][4:8], halves[1][4:8]]
    h_out[...] = jnp.concatenate(lines, axis=0).astype(BF16)

    def settle(head, carry):
        for d in range(1, 4):
            deliver(d, head).wait_recv()
        keep(head).wait()
        return carry

    lax.fori_loop(0, HD, settle, 0)
    for array, out in ((0, q_out), (1, k_out), (2, v_out)):
        out[...] = back[array]

    for array in range(4):
        for head in range(HD):
            peer_copy(array, head).wait_send()
    for d in range(2):
        for slot in range(CAP[d]):
            if d + slot > 0:
                forward(d, slot).wait_send()
            give_back(d, slot).wait_send()
    for array in range(4):
        edge_copy(array).wait_send()
    for head in range(HD):
        for d in range(1, 4):
            deliver(d, head).wait_send()
    for kind in range(5):
        meta_copy(kind).wait_send()
    for d in range(1, 8):
        row_y(d).wait_send()
        row_z(d).wait_send()
        out_y(d).wait_send()
        out_z(d).wait_send()
    for d in range(1, 4):
        row_x(d).wait_send()
        out_x(d).wait_send()


def finish(q_in, k_in, v_in, h_in, q_out, k_out, v_out, hk_out, hv_out):
    q_out[...] = q_in[...]
    k_out[...] = k_in[...]
    v_out[...] = v_in[...]
    rows = h_in[...].astype(F32)
    for i in range(8):
        hk_out[:, DH * i : DH * i + DH] = rows[i : i + 1].astype(BF16)
        hv_out[:, DH * i : DH * i + DH] = rows[8 + i : 9 + i].astype(BF16)


def body(
    queries, key_rows, value_rows, out_grad, padding, header_keys, header_values,
    neighbours, slot_valid, crystal_ids, header_index,
):
    grad = jax.ShapeDtypeStruct((BLK, 2048), BF16)
    vmem = pl.BlockSpec(memory_space=pltpu.VMEM)
    hbm = pl.BlockSpec(memory_space=pl.ANY)
    dma = pltpu.SemaphoreType.DMA
    q_grad, k_grad, v_grad, h_grad = pl.pallas_call(
        kernel,
        out_shape=(grad, grad, grad, jax.ShapeDtypeStruct((16, DH), BF16)),
        in_specs=[hbm] * 4 + [vmem] * 3 + [pl.BlockSpec(memory_space=pltpu.SMEM)] * 4,
        out_specs=[vmem] * 4,
        scratch_shapes=[
            pltpu.VMEM((HD, 4, 4, BLK, DH), BF16),
            pltpu.VMEM((10, 4, BLK, DH), BF16),
            pltpu.VMEM((10, 4, BLK, DH), BF16),
            pltpu.VMEM((10, 4, BLK, DH), BF16),
            pltpu.VMEM((2, 2, ROWS, DH), BF16),
            pltpu.VMEM((2, 2, KEYS, DH), BF16),
            pltpu.VMEM((2, KEYS, ROWS), BF16),
            pltpu.VMEM((2, KEYS, ROWS), BF16),
            pltpu.VMEM((2, KEYS, BLK), F32),
            pltpu.VMEM((2, HD, 3, MOST, BLK, DH), BF16),
            pltpu.VMEM((10, 3, BLK, DH), BF16),
            pltpu.VMEM((10, 3, BLK, DH), BF16),
            pltpu.VMEM((10, 3, BLK, DH), BF16),
            pltpu.VMEM((HD, 4, 3, BLK, DH), BF16),
            pltpu.VMEM((3, BLK, 2048), BF16),
            pltpu.VMEM((6, 8, BLK), jnp.int32),
            pltpu.SMEM((6, 8, BLK), jnp.int32),
            pltpu.VMEM((12, 8, BLK), F32),
            pltpu.VMEM((8, 16, DH), BF16),
            pltpu.VMEM((SEQ // 2, 16, DH), BF16),
            pltpu.VMEM((4, 8, DH), F32),
            pltpu.VMEM((4, 8, DH), F32),
            pltpu.VMEM((8, 48, DH), BF16),
            pltpu.VMEM((4, 8 * 48, DH), BF16),
            pltpu.VMEM((8, 8, DH), F32),
            pltpu.VMEM((8, 8, DH), F32),
            dma((HD, 4)),
            dma((HD, 4)),
            dma((HD, 4)),
            dma((10,)),
            dma((10,)),
            dma((10,)),
            dma((10,)),
            dma((HD, 3)),
            dma((HD, 3)),
            dma((HD,)),
            dma((4,)),
            dma((4,)),
            dma((5,)),
            dma((6,)),
            dma,
            dma((17,)),
            dma((17,)),
            dma((17,)),
            dma((17,)),
        ],
        compiler_params=pltpu.CompilerParams(
            collective_id=0, has_side_effects=True, vmem_limit_bytes=56 * 1024 * 1024
        ),
    )(*[each.reshape(2, BLK, 1024) for each in (queries, out_grad, key_rows, value_rows)], padding.reshape(2, BLK), header_keys, header_values,
      neighbours, slot_valid, crystal_ids, header_index.T)
    line = jax.ShapeDtypeStruct((1, 1024), BF16)
    return pl.pallas_call(
        finish,
        out_shape=(grad, grad, grad, line, line),
        compiler_params=pltpu.CompilerParams(vmem_limit_bytes=56 * 1024 * 1024),
    )(q_grad, k_grad, v_grad, h_grad)


def solution(mesh):
    in_specs = (
        P("seq", "head"),
        P("seq", "head"),
        P("seq", "head"),
        P("seq", "head"),
        P("seq"),
        P("seq", "head"),
        P("seq", "head"),
        P("seq", None),
        P("seq", None),
        P("seq"),
        P(),
    )
    out_specs = (
        P(("seq", "head"), None),
        P(("seq", "head"), None),
        P(("seq", "head"), None),
        P("seq", "head"),
        P("seq", "head"),
    )
    return jax.shard_map(body, mesh=mesh, in_specs=in_specs, out_specs=out_specs, check_vma=False)
```

```python
import math

import jax
import jax.numpy as jnp
from jax import lax
from jax.experimental import pallas as pl
from jax.experimental.pallas import tpu as pltpu
from jax.sharding import PartitionSpec as P

DH = 128
BLK = 128
NEG = -1e30
FACTOR = 1.0 / math.sqrt(DH)
F32 = jnp.float32
BF16 = jnp.bfloat16
HD = 4
MOST = 5
ROWS = MOST * BLK
KEYS = ROWS + 16
SEQ = 256
CAP = (6, 4)
CHUNKS = ((0, 384), (384, 640))


def kernel(
    q_in, g_in, k_in, v_in, pad_in, hk_in, hv_in, lists, valid, ids, hidx,
    q_out, k_out, v_out, h_out,
    wk, sbuf, land, imp, cqg, ckv, probs, mixes, bias, gr, rsend, rland, rw, ost, back,
    meta, meta_s, padw, tabf, table, hb, hd, hz, hx, hs, ry,
    e_send, e_recv, own_sem, f_send, f_recv, r_send, r_recv, x_send, x_recv, xown_sem,
    m_send, m_recv, ms_sem, hs_send, hs_recv, ht_send, ht_recv,
):
    e = lax.axis_index("seq")
    h = lax.axis_index("head")
    core = lax.rem(e, 2)
    chip = e // 2
    j8 = lax.rem(e, 8)
    x4 = lax.rem(e // 8, 4)
    z8 = e // 32

    def wrap(index):
        return lax.rem(index + SEQ, SEQ)

    step = 2 * core - 1
    peer = e + 1 - 2 * core
    sends_to = (wrap(e + 2 * step), wrap(e - 2 * step))
    comes_from = (sends_to[1], sends_to[0])
    left, right = wrap(2 * chip - 2), wrap(2 * chip + 2)

    def y_peer(d):
        return e - j8 + lax.rem(j8 + d, 8)

    def x_peer(d):
        return e - 8 * x4 + 8 * lax.rem(x4 + d, 4)

    def z_peer(d):
        return e - 32 * z8 + 32 * lax.rem(z8 + d, 8)

    barrier = pltpu.get_barrier_semaphore()

    def greet(device, other):
        pl.semaphore_signal(barrier, inc=1, device_id=(device, other), device_id_type=pl.DeviceIdType.MESH)

    for d in range(1, 8):
        greet(y_peer(d), h)
        greet(z_peer(d), h)
    for d in range(1, 4):
        greet(x_peer(d), h)
    for c in range(2):
        greet(left + c, h)
        greet(right + c, h)
    greet(e, 1 - h)
    greet(peer, 1 - h)

    def remote(src, dst, send, recv, device, other):
        return pltpu.make_async_remote_copy(
            src_ref=src, dst_ref=dst, send_sem=send, recv_sem=recv,
            device_id=(device, other), device_id_type=pl.DeviceIdType.MESH,
        )

    ins = (q_in, g_in, k_in, v_in)

    def own_copy(array, head):
        cols = pl.ds(pl.multiple_of((core * HD + head) * DH, DH), DH)
        there = wk.at[head, array, pl.ds(2 * core, 2)]
        return pltpu.make_async_copy(ins[array].at[:, :, cols], there, own_sem.at[head, array])

    def peer_copy(array, head):
        cols = pl.ds(pl.multiple_of(((1 - core) * HD + head) * DH, DH), DH)
        there = wk.at[head, array, pl.ds(2 * core, 2)]
        return remote(ins[array].at[:, :, cols], there, e_send.at[head, array], e_recv.at[head, array], peer, h)

    for array in range(4):
        for head in range(HD):
            own_copy(array, head).start()
    lines = [each[:, DH * i : DH * i + DH] for each in (hk_in, hv_in) for i in range(8)]
    tabf[pl.ds(j8, 1)] = jnp.concatenate([line.astype(F32) for line in lines], axis=0).astype(BF16)[None]
    starts, sizes = [], []
    for block in range(2):
        first, size = jnp.int32(1 << 20), jnp.int32(0)
        for slot in range(MOST):
            used = valid[block, slot] > 0
            first = jnp.where(used, jnp.minimum(first, lists[block, slot]), first)
            size = size + jnp.where(used, 1, 0)
        starts.append(first)
        sizes.append(size)
    lines = [jnp.full((1, BLK), each, jnp.int32) for each in starts + sizes + [ids[0], ids[1]]]
    meta[pl.ds(2 + core, 1)] = jnp.concatenate([pad_in[...]] + lines, axis=0)[None]

    pl.semaphore_wait(barrier, 23)

    meta_to = ((peer, 2 + core), (left, 4 + core), (left + 1, 4 + core), (right, core), (right + 1, core))

    def meta_copy(kind):
        device, slot = meta_to[kind]
        return remote(meta.at[2 + core], meta.at[slot], m_send.at[kind], m_recv.at[slot], device, h)

    def meta_arrival(slot):
        return remote(meta.at[2 + core], meta.at[slot], m_send.at[0], m_recv.at[slot], peer, h)


    def row_y(d):
        return remote(tabf.at[j8], tabf.at[j8], hs_send.at[d - 1], hs_recv.at[d - 1], y_peer(d), h)

    def row_x(d):
        part = table.at[pl.ds(4 * (4 * z8 + x4), 4)]
        return remote(part, part, hs_send.at[6 + d], hs_recv.at[6 + d], x_peer(d), h)

    def row_z(d):
        part = table.at[pl.ds(16 * z8, 16)]
        return remote(part, part, hs_send.at[9 + d], hs_recv.at[9 + d], z_peer(d), h)

    for d in range(1, 8):
        row_y(d).start()
    for kind in range(5):
        meta_copy(kind).start()
    for array in range(4):
        for head in range(HD):
            peer_copy(array, head).start()

    for d in range(1, 8):
        row_y(d).wait_recv()
    rows = tabf[...].astype(F32)
    halves = [
        jnp.concatenate([rows[:, HD * c : HD * c + HD], rows[:, 8 + HD * c : 8 + HD * c + HD]], axis=1)
        for c in range(2)
    ]
    rows = jnp.where(core == 0, halves[0], halves[1])
    table[pl.ds(4 * (4 * z8 + x4), 4)] = rows.reshape(4, 16, DH).astype(BF16)
    for d in range(1, 4):
        row_x(d).start()

    for slot in (0, 1, 4, 5):
        meta_arrival(slot).wait_recv()
    meta_arrival(3 - core).wait_recv()
    to_scalar = pltpu.make_async_copy(meta, meta_s, ms_sem)
    to_scalar.start()
    for d in range(1, 4):
        row_x(d).wait_recv()
    for d in range(1, 8):
        row_z(d).start()
    to_scalar.wait()
    start_x, size_x, id_x = meta_s[2, 2, 0] - 4 * chip, meta_s[2, 4, 0], meta_s[2, 6, 0]
    start_y, size_y, id_y = meta_s[3, 3, 0] - 4 * chip, meta_s[3, 5, 0], meta_s[3, 7, 0]
    a_x = jnp.maximum(-start_x, 0)
    b_x = size_x - a_x
    b_y = jnp.maximum(start_y + size_y - 4, 0)
    a_y = size_y - b_y
    cross_x, cross_y = a_x > 0, b_y > 0
    same = id_x == id_y
    on_x = jnp.logical_not(same & cross_y)
    on_y = jnp.logical_not(same) | cross_y

    def left_heads(a, b):
        return jnp.where(b == 1, 3, jnp.where(a == 1, 1, jnp.where(b == 2, 3 - core, 2 - core)))

    split_x, split_y = left_heads(a_x, b_x), left_heads(a_y, b_y)

    def home_x(head):
        return jnp.logical_not(cross_x) | (head >= split_x)

    def home_y(head):
        return jnp.logical_not(cross_y) | (head < split_y)

    is_x = (core == 1, core == 0)

    def pick(unit, of_x, of_y):
        return jnp.where(is_x[unit], of_x, of_y)

    start_u = [pick(u, start_x, start_y) for u in range(2)]
    size_u = [pick(u, size_x, size_y) for u in range(2)]
    width_u = [pick(u, a_x, b_y) for u in range(2)]
    given_u = [pick(u, b_x, a_y) for u in range(2)]
    id_u = [pick(u, id_x, id_y) for u in range(2)]
    on_u = [pick(u, on_x, on_y) for u in range(2)]

    def over(slot, width):
        by = [slot // n for n in range(1, 5)]
        return jnp.where(width == 2, by[1], jnp.where(width == 3, by[2], jnp.where(width == 4, by[3], by[0])))

    def rest(slot, width):
        return slot - over(slot, width) * jnp.clip(width, 1, 4)

    for array in range(4):
        for head in range(HD):
            own_copy(array, head).wait()
            peer_copy(array, head).wait_recv()

    def forward(d, slot):
        at = 6 * d + slot
        return remote(sbuf.at[at], land.at[at], f_send.at[at], f_recv.at[at], sends_to[d], h)

    def send(d, slot):
        unit = 1 - d
        width = given_u[unit]
        order = jnp.clip(over(slot, width), 0, HD - 1)
        part = rest(slot, width)
        head = pick(unit, order, HD - 1 - order)
        block = jnp.clip(pick(unit, part, 4 - a_y + part), 0, 3)
        sbuf[6 * d + slot] = wk[head, :, block]
        forward(d, slot).start()

    for slot in range(4):
        for d in range(2):
            send(d, slot)
    for slot in range(4, 6):
        send(0, slot)

    for slot in range(6):
        for block in range(2):
            padw[2 * slot + block] = jnp.broadcast_to(meta[slot, block : block + 1, :].astype(F32), (8, BLK))
    for u in range(2):
        for p in range(MOST):
            line = padw[jnp.clip(start_u[u] + p + 4, 0, 11)][0:1]
            full = jnp.broadcast_to(line, (BLK, BLK)).T
            full = jnp.where(p < size_u[u], full, 0.0)
            bias[u, p * BLK : p * BLK + BLK, :] = jnp.where(full > 0.0, 0.0, NEG)
        at = lax.broadcasted_iota(jnp.int32, (16, BLK), 0)
        bias[u, ROWS:KEYS, :] = jnp.where(at < 2, 0.0, NEG)

    for d in range(1, 8):
        row_z(d).wait_recv()
    names = []
    for u in range(2):
        for slot in range(2):
            row = hidx[slot, id_u[u]]
            pair = table[lax.div(row, 2)].astype(F32)
            hb[2 * u + slot] = jnp.where(lax.rem(row, 2) == 0, pair[0:8], pair[8:16])
            names.append(jnp.where(on_u[u], row, -1))

    def nt(a, b):
        return lax.dot_general(a, b, (((1,), (1,)), ((), ())), preferred_element_type=F32)

    def give_back(d, slot):
        at = 6 * d + slot
        return remote(rsend.at[at], rland.at[at], r_send.at[at], r_recv.at[at], comes_from[d], h)

    def send_back(d, slot):
        part = rest(slot, width_u[d])
        turn = jnp.clip(over(slot, width_u[d]), 0, HD - 1)
        p = jnp.clip(pick(d, part, part + 4 - start_u[d]), 0, MOST - 1)
        rsend[6 * d + slot] = gr[d, turn, :, p]
        give_back(d, slot).start()

    def work(turn, carry):
        @pl.when(turn == 0)
        def _():
            for slot in range(4):
                for d in range(2):
                    forward(d, slot).wait_recv()
                    imp[6 * d + slot] = land[6 * d + slot]

        @pl.when(turn == 1)
        def _():
            for slot in range(4, 6):
                forward(0, slot).wait_recv()
                imp[slot] = land[slot]

        for u in range(2):
            head = turn + (core if u == 0 else 1 - core) * (HD - 1 - 2 * turn)
            last = jnp.where(turn == 0, 3, CAP[u] - 1)
            for p in range(MOST):
                there = start_u[u] + p
                slot = turn * width_u[u] + pick(u, p, there - 4)
                outside = (there < 0) | (there > 3)
                far = imp[6 * u + jnp.clip(slot, 0, last)]
                near = wk[head, :, jnp.clip(there, 0, 3)]
                rows = jnp.where(outside, far, near)
                span = slice(p * BLK, p * BLK + BLK)
                cqg[u, :, span, :] = jnp.where(p < size_u[u], rows[0:2], jnp.zeros_like(rows[0:2]))
                ckv[u, :, span, :] = rows[2:4]
            for array in range(2):
                at = pl.ds(array * HD + head, 1)
                lines = [hb[2 * u + slot, at, :] for slot in range(2)] + [jnp.zeros((14, DH), F32)]
                ckv[u, array, ROWS:KEYS, :] = jnp.concatenate(lines, axis=0).astype(BF16)
            for lo, hi in CHUNKS:
                q = cqg[u, 0, lo:hi, :]
                g = cqg[u, 1, lo:hi, :]
                keys = ckv[u, 0]
                values = ckv[u, 1]
                mask = bias[u]
                mask = jnp.concatenate([mask] * ((hi - lo) // BLK), axis=1)
                score = nt(keys, q) * FACTOR + mask
                top = jnp.max(score, axis=0, keepdims=True)
                grown = jnp.exp(score - top)
                prob = grown * (1.0 / jnp.sum(grown, axis=0, keepdims=True))
                low = prob.astype(BF16)
                dprob = nt(values, g)
                delta = jnp.sum(low.astype(F32) * dprob, axis=0, keepdims=True)
                mixing = (FACTOR * prob * (dprob - delta)).astype(BF16)
                probs[u, :, lo:hi] = low
                mixes[u, :, lo:hi] = mixing
                q_grad = lax.dot_general(mixing, keys, (((0,), (0,)), ((), ())), preferred_element_type=F32)
                gr[u, turn, 0, lo // BLK : hi // BLK] = q_grad.astype(BF16).reshape(-1, BLK, DH)
            here = pick(u, home_x(head), home_y(head))
            for array, weights in ((0, mixes), (1, probs)):
                total = jnp.dot(weights[u], cqg[u, array], preferred_element_type=F32)
                gr[u, turn, 1 + array] = total[0:ROWS].astype(BF16).reshape(MOST, BLK, DH)
                for slot in range(2):
                    line = total[ROWS + slot : ROWS + slot + 1]
                    hd[2 * u + slot, pl.ds(array * HD + head, 1), :] = jnp.where(here, line, 0.0)

        for ready, slots in ((0, (0,)), (1, (1, 3)), (2, (2, 4, 5))):

            @pl.when(turn == ready)
            def _(slots=slots):
                for slot in slots:
                    for d in range(2):
                        if slot < CAP[d]:
                            send_back(d, slot)

        return carry

    lax.fori_loop(0, HD, work, 0)

    tags = [jnp.full((1, DH), name).astype(F32) for name in names] + [jnp.full((12, DH), -1.0, F32)]
    block = jnp.concatenate([hd[slot] for slot in range(4)] + tags, axis=0)
    hz[pl.ds(z8, 1)] = block.astype(BF16)[None]

    def out_z(d):
        return remote(hz.at[z8], hz.at[z8], ht_send.at[d - 1], ht_recv.at[d - 1], z_peer(d), h)

    def out_x(d):
        return remote(hx.at[x4], hx.at[x4], ht_send.at[6 + d], ht_recv.at[6 + d], x_peer(d), h)

    def out_y(d):
        src = hs.at[lax.rem(j8 + d, 8)]
        return remote(src, ry.at[j8], ht_send.at[9 + d], ht_recv.at[9 + d], y_peer(d), h)

    for d in range(1, 8):
        out_z(d).start()

    mine = 2 * core + h

    def column(head):
        return pl.ds(pl.multiple_of(h * 1024 + (core * HD + head) * DH, DH), DH)

    def deliver(d, head):
        there = lax.rem(mine + d, 4)
        return remote(
            ost.at[head, there], back.at[:, :, column(head)], x_send.at[head, d - 1], x_recv.at[head, d - 1],
            2 * chip + there // 2, lax.rem(there, 2),
        )

    def keep(head):
        return pltpu.make_async_copy(ost.at[head, mine], back.at[:, :, column(head)], xown_sem.at[head])

    for slot in range(4):
        for d in range(2):
            give_back(d, slot).wait_recv()
            rw[6 * d + slot] = rland[6 * d + slot]
    unit_x = jnp.where(core == 1, 0, 1)

    def assemble(head, carry):
        for j in range(4):
            in_x = on_x & (j < start_x + size_x)
            unit = jnp.where(in_x, unit_x, 1 - unit_x)
            when = jnp.where(in_x, HD - 1 - head, head)
            p = jnp.clip(jnp.where(in_x, j - start_x, j - start_y), 0, MOST - 1)
            slot = jnp.where(in_x, head * b_x + j, (HD - 1 - head) * a_y + j - start_y)
            here = jnp.where(in_x, home_x(head).astype(jnp.int32), home_y(head).astype(jnp.int32)) > 0
            most = jnp.where(unit == 1, CAP[0] - 1, CAP[1] - 1)
            at = 6 * (1 - unit) + jnp.clip(slot, 0, most)
            worked = gr[unit, when, :, p]
            ost[head, j] = jnp.where(here, worked, rw[at])
        for d in range(1, 4):
            deliver(d, head).start()
        keep(head).start()
        return carry

    def assemble_pair(one, two):
        lax.fori_loop(0, 2, lambda i, carry: assemble(one + (two - one) * i, carry), 0)

    assemble_pair(0, 3)
    for slot in range(4, 6):
        give_back(0, slot).wait_recv()
        rw[slot] = rland[slot]
    assemble_pair(1, 2)

    for d in range(1, 8):
        out_z(d).wait_recv()
    hx[pl.ds(x4, 1)] = hz[...].reshape(1, 8 * 48, DH)
    for d in range(1, 4):
        out_x(d).start()
    for d in range(1, 4):
        out_x(d).wait_recv()
    first = 32 * z8 + 8 * x4

    def gather(at, totals):
        block = hx[at // 8, pl.ds(pl.multiple_of(lax.rem(at, 8) * 48, 16), 48), :].astype(F32)
        totals = list(totals)
        for slot in range(4):
            tag = jnp.broadcast_to(block[32 + slot : 33 + slot], (8, DH)) - first.astype(F32)
            for j in range(8):
                totals[j] = totals[j] + jnp.where(tag == float(j), block[8 * slot : 8 * slot + 8], 0.0)
        return tuple(totals)

    totals = lax.fori_loop(0, 32, gather, tuple(jnp.zeros((8, DH), F32) for _ in range(8)))
    for j in range(8):
        hs[j] = totals[j]
    for d in range(1, 8):
        out_y(d).start()
    ry[pl.ds(j8, 1)] = hs[pl.ds(j8, 1)]
    for d in range(1, 8):
        out_y(d).wait_recv()
    halves = [ry[c] + ry[c + 2] + ry[c + 4] + ry[c + 6] for c in range(2)]
    lines = [halves[0][0:4], halves[1][0:4], halves[0][4:8], halves[1][4:8]]
    h_out[...] = jnp.concatenate(lines, axis=0).astype(BF16)

    def settle(head, carry):
        for d in range(1, 4):
            deliver(d, head).wait_recv()
        keep(head).wait()
        return carry

    lax.fori_loop(0, HD, settle, 0)
    for array, out in ((0, q_out), (1, k_out), (2, v_out)):
        out[...] = back[array]

    for array in range(4):
        for head in range(HD):
            peer_copy(array, head).wait_send()
    for d in range(2):
        for slot in range(CAP[d]):
            forward(d, slot).wait_send()
            give_back(d, slot).wait_send()
    for head in range(HD):
        for d in range(1, 4):
            deliver(d, head).wait_send()
    for kind in range(5):
        meta_copy(kind).wait_send()
    for d in range(1, 8):
        row_y(d).wait_send()
        row_z(d).wait_send()
        out_y(d).wait_send()
        out_z(d).wait_send()
    for d in range(1, 4):
        row_x(d).wait_send()
        out_x(d).wait_send()


def finish(q_in, k_in, v_in, h_in, q_out, k_out, v_out, hk_out, hv_out):
    q_out[...] = q_in[...]
    k_out[...] = k_in[...]
    v_out[...] = v_in[...]
    rows = h_in[...].astype(F32)
    for i in range(8):
        hk_out[:, DH * i : DH * i + DH] = rows[i : i + 1].astype(BF16)
        hv_out[:, DH * i : DH * i + DH] = rows[8 + i : 9 + i].astype(BF16)


def body(
    queries, key_rows, value_rows, out_grad, padding, header_keys, header_values,
    neighbours, slot_valid, crystal_ids, header_index,
):
    grad = jax.ShapeDtypeStruct((BLK, 2048), BF16)
    vmem = pl.BlockSpec(memory_space=pltpu.VMEM)
    hbm = pl.BlockSpec(memory_space=pl.ANY)
    dma = pltpu.SemaphoreType.DMA
    q_grad, k_grad, v_grad, h_grad = pl.pallas_call(
        kernel,
        out_shape=(grad, grad, grad, jax.ShapeDtypeStruct((16, DH), BF16)),
        in_specs=[hbm] * 4 + [vmem] * 3 + [pl.BlockSpec(memory_space=pltpu.SMEM)] * 4,
        out_specs=[vmem] * 4,
        scratch_shapes=[
            pltpu.VMEM((HD, 4, 4, BLK, DH), BF16),
            pltpu.VMEM((10, 4, BLK, DH), BF16),
            pltpu.VMEM((10, 4, BLK, DH), BF16),
            pltpu.VMEM((10, 4, BLK, DH), BF16),
            pltpu.VMEM((2, 2, ROWS, DH), BF16),
            pltpu.VMEM((2, 2, KEYS, DH), BF16),
            pltpu.VMEM((2, KEYS, ROWS), BF16),
            pltpu.VMEM((2, KEYS, ROWS), BF16),
            pltpu.VMEM((2, KEYS, BLK), F32),
            pltpu.VMEM((2, HD, 3, MOST, BLK, DH), BF16),
            pltpu.VMEM((10, 3, BLK, DH), BF16),
            pltpu.VMEM((10, 3, BLK, DH), BF16),
            pltpu.VMEM((10, 3, BLK, DH), BF16),
            pltpu.VMEM((HD, 4, 3, BLK, DH), BF16),
            pltpu.VMEM((3, BLK, 2048), BF16),
            pltpu.VMEM((6, 8, BLK), jnp.int32),
            pltpu.SMEM((6, 8, BLK), jnp.int32),
            pltpu.VMEM((12, 8, BLK), F32),
            pltpu.VMEM((8, 16, DH), BF16),
            pltpu.VMEM((SEQ // 2, 16, DH), BF16),
            pltpu.VMEM((4, 8, DH), F32),
            pltpu.VMEM((4, 8, DH), F32),
            pltpu.VMEM((8, 48, DH), BF16),
            pltpu.VMEM((4, 8 * 48, DH), BF16),
            pltpu.VMEM((8, 8, DH), F32),
            pltpu.VMEM((8, 8, DH), F32),
            dma((HD, 4)),
            dma((HD, 4)),
            dma((HD, 4)),
            dma((10,)),
            dma((10,)),
            dma((10,)),
            dma((10,)),
            dma((HD, 3)),
            dma((HD, 3)),
            dma((HD,)),
            dma((5,)),
            dma((6,)),
            dma,
            dma((17,)),
            dma((17,)),
            dma((17,)),
            dma((17,)),
        ],
        compiler_params=pltpu.CompilerParams(
            collective_id=0, has_side_effects=True, vmem_limit_bytes=56 * 1024 * 1024
        ),
    )(*[each.reshape(2, BLK, 1024) for each in (queries, out_grad, key_rows, value_rows)], padding.reshape(2, BLK), header_keys, header_values,
      neighbours, slot_valid, crystal_ids, header_index.T)
    line = jax.ShapeDtypeStruct((1, 1024), BF16)
    return pl.pallas_call(
        finish,
        out_shape=(grad, grad, grad, line, line),
        compiler_params=pltpu.CompilerParams(vmem_limit_bytes=56 * 1024 * 1024),
    )(q_grad, k_grad, v_grad, h_grad)


def solution(mesh):
    in_specs = (
        P("seq", "head"),
        P("seq", "head"),
        P("seq", "head"),
        P("seq", "head"),
        P("seq"),
        P("seq", "head"),
        P("seq", "head"),
        P("seq", None),
        P("seq", None),
        P("seq"),
        P(),
    )
    out_specs = (
        P(("seq", "head"), None),
        P(("seq", "head"), None),
        P(("seq", "head"), None),
        P("seq", "head"),
        P("seq", "head"),
    )
    return jax.shard_map(body, mesh=mesh, in_specs=in_specs, out_specs=out_specs, check_vma=False)
```
